32 devices in a mesh: dp: 8 (over z, y), mp: 4 (over x, core).
Axes of the slice: x: 2, y: 2, z: 4, core: 2. Of those that a mesh axis runs over, the one named last changes fastest.
Arguments:
- current: bfloat16 [5120, 768], P('dp', 'mp'), may hold values from -6 to 6
- history: bfloat16 [12, 5120, 768], P(None, 'dp', 'mp'), may hold values from -6 to 6
- cotangent: bfloat16 [5120, 768], P('dp', 'mp'), may hold values from -15.3 to 15.3
- seq_lengths: int32 [8, 4], P('dp'), may hold values from 1 to 512, 640 in all within a row
- w_qkv: bfloat16 [2, 768, 2304], P(None, None, 'mp'), may hold values from -0.21875 to 0.21875
- w_out: bfloat16 [2, 768, 768], P(None, 'mp'), may hold values from -0.875 to 0.875
- w_up: bfloat16 [2, 768, 3072], P(None, None, 'mp'), may hold values from -0.21875 to 0.21875
- w_down: bfloat16 [2, 3072, 768], P(None, 'mp'), may hold values from -0.109375 to 0.109375
- gain_attn: float32 [2, 768], replicated, may hold values from 0.5 to 1.5
- gain_mlp: float32 [2, 768], replicated, may hold values from 0.5 to 1.5
- dwa_first: float32 [13], replicated, may hold values from 0.1 to 0.6
- dwa_second: float32 [14], replicated, may hold values from 0.1 to 0.6
Outputs:
- mixed: bfloat16 [5120, 768], P('dp', 'mp')
- grad_current: bfloat16 [5120, 768], P('dp', 'mp')
- grad_history: bfloat16 [12, 5120, 768], P(None, 'dp', 'mp')
- grad_qkv: float32 [2, 768, 2304], P(None, 'dp', 'mp')
- grad_out: float32 [2, 768, 768], P(None, 'mp', 'dp')
- grad_up: float32 [2, 768, 3072], P(None, 'dp', 'mp')
- grad_down: float32 [2, 3072, 768], P(None, 'mp', 'dp')
- grad_gain_attn: float32 [2, 768], replicated
- grad_gain_mlp: float32 [2, 768], replicated
- grad_dwa_first: float32 [13], replicated
- grad_dwa_second: float32 [14], replicated
The draws below stay inside these ranges and needn't reach their ends.
Inputs may be any that keep to these rules, and one draw needn't show every extreme that they name: `seq_lengths`: each row sums to 640, and its largest entry is 512.
All inputs are finite; a program needn't handle non-finite values.
Results may differ from the reference program's by a relative error of at most 0.025.
Values may be sent and summed in bfloat16 or wider, within the bound.
A program may use at most 192 MiB of HBM per device.

```python
import math
import jax
import jax.numpy as jnp
import numpy as np
from jax import lax

D = 768
HEADS = 12
HEAD_DIM = 64
FF = 3072
LAYERS = 2
PAST = 12
SEGS = 4
TOK_DEV = 640
LONGEST = 512
TOKENS = 5120
N_DP = 8


def draw_cotangent(key, part):
    key = jax.random.fold_in(key, 7)
    places = jnp.arange(TOKENS, dtype=jnp.float32) / TOKENS
    base = jnp.clip(jax.random.normal(key, (TOKENS, D), jnp.float32), -5.0, 5.0)
    scale = 3.0 ** places
    return (base * scale[:, None]).astype(jnp.bfloat16)


def level_of(rng, shape, split, low, top_value):
    level, own = 1.0, jax.random.fold_in(rng, 6)
    for dim, shards_of in split:
        heights = jnp.exp(jax.random.uniform(jax.random.fold_in(own, dim), (shards_of,), jnp.float32, low / len(split), top_value / len(split)))
        level = level * jnp.repeat(heights, shape[dim] // shards_of).reshape([-1 if axis == dim else 1 for axis in range(len(shape))])
    return level


def profile(count, total, reach, slope):
    weights = [(1 << 20) // math.isqrt(rank ** slope) + 1 for rank in range(2, count + 1)]
    surplus, counts = total - reach - (count - 1), [1] * (count - 1)
    while surplus > 0:
        free = [i for i in range(count - 1) if counts[i] < reach]
        whole, budget = sum([weights[i] for i in free]), surplus
        for i in free:
            addition = min(reach - counts[i], max(1, budget * weights[i] // whole), surplus)
            counts[i] = counts[i] + addition
            surplus = surplus - addition
    return np.array([reach] + counts)


def ragged_sizes(rng, count, total, limit, lean):
    if count == 2:
        one = jax.random.randint(rng, (), max(1, total - limit), min(limit, total - 1) + 1)
        return jnp.stack([one, total - one])
    sizes = jnp.asarray(profile(count, total, limit, lean), jnp.int32)
    pairs = (count - 1) // 2
    giver, sink = sizes[1:1 + 2 * pairs:2], sizes[2:2 + 2 * pairs:2]
    slack = jnp.minimum(giver - 1, limit - sink)
    shifted = jax.random.randint(jax.random.fold_in(rng, 1), (pairs,), 0, 1 << 20) % (slack + 1)
    sizes = sizes.at[1:1 + 2 * pairs:2].set(giver - shifted).at[2:2 + 2 * pairs:2].set(sink + shifted)
    return sizes[jax.random.permutation(jax.random.fold_in(rng, 2), count)]


def gaussian(own_key, extent, width, bound, shards=(), kind=jnp.bfloat16):
    values = width * jax.random.normal(own_key, extent, jnp.float32)
    if shards:
        values = values * level_of(own_key, extent, shards, -0.22, 0.18)
    return jnp.clip(values, -bound, bound).astype(kind)


def setup_inputs(seed: int = 0) -> dict:
    arg_keys = jax.random.split(jax.random.key(seed), 13)
    current = gaussian(arg_keys[0], (TOKENS, D), 1.0, 6.0, ((0, 8), (1, 4)))
    history = gaussian(arg_keys[1], (PAST, TOKENS, D), 1.0, 6.0, ((1, 8), (2, 4)))
    cotangent = draw_cotangent(jax.random.fold_in(arg_keys[12], 71), 0)
    seq_lengths = jax.vmap(lambda own: ragged_sizes(own, SEGS, TOK_DEV, LONGEST, 2))(jax.random.split(arg_keys[3], N_DP)).reshape((N_DP, SEGS)).astype(jnp.int32)
    w_qkv = gaussian(arg_keys[4], (LAYERS, D, 3 * D), D ** -0.5, 0.21875, ((2, 4),))
    w_out = gaussian(arg_keys[5], (LAYERS, D, D), (D // 16) ** -0.5, 0.875, ((1, 4),))
    w_up = gaussian(arg_keys[6], (LAYERS, D, FF), D ** -0.5, 0.21875, ((2, 4),))
    w_down = gaussian(arg_keys[7], (LAYERS, FF, D), FF ** -0.5, 0.109375, ((1, 4),))
    gain_attn = jnp.clip(1.0 + 0.1 * jax.random.normal(arg_keys[8], (LAYERS, D), jnp.float32), 0.5, 1.5)
    gain_mlp = jnp.clip(1.0 + 0.1 * jax.random.normal(arg_keys[9], (LAYERS, D), jnp.float32), 0.5, 1.5)
    dwa_first = jnp.clip(jax.random.uniform(arg_keys[10], (PAST + 1,), jnp.float32, 0.1, 0.6), 0.1, 0.6)
    dwa_second = jnp.clip(jax.random.uniform(arg_keys[11], (PAST + 2,), jnp.float32, 0.1, 0.6), 0.1, 0.6)
    return {"current": current, "history": history, "cotangent": cotangent, "seq_lengths": seq_lengths, "w_qkv": w_qkv, "w_out": w_out, "w_up": w_up, "w_down": w_down, "gain_attn": gain_attn, "gain_mlp": gain_mlp, "dwa_first": dwa_first, "dwa_second": dwa_second}


@jax.custom_vjp
def low(v):
    return lax.optimization_barrier(v.astype(jnp.bfloat16)).astype(jnp.float32)

@jax.custom_vjp
def low_back(v):
    return v

def low_keep(v):
    return (low(v), None)

def low_pass(kept, grad):
    return (grad,)

def back_keep(v):
    return (v, None)

def back_low(kept, grad):
    return (low(grad),)
low.defvjp(low_keep, low_pass)
low_back.defvjp(back_keep, back_low)
epsilon = 1e-05

def normalize(values, gain):
    center = values - lax.optimization_barrier(jnp.mean(values, -1, keepdims=True))
    spread = lax.optimization_barrier(jnp.mean(center * center, -1, keepdims=True))
    return center * lax.rsqrt(spread + epsilon) * gain

def tables(lengths, rows, head_dim):
    ends = jnp.cumsum(lengths).astype(jnp.int32)
    places = jnp.arange(rows, dtype=jnp.int32)
    passed = (places[:, None] >= ends[None, :]).astype(jnp.int32)
    segment = lax.optimization_barrier(jnp.sum(passed, 1))
    starts = lax.optimization_barrier(jnp.sum(passed * lengths[None, :], 1))
    offset = (places - starts).astype(jnp.float32)
    visible = (segment[:, None] == segment[None, :]) & (places[None, :] <= places[:, None])
    freqs = 10000.0 ** (-2.0 * jnp.arange(head_dim // 2, dtype=jnp.float32) / head_dim)
    angles = offset[:, None] * freqs[None, :]
    return (visible, jnp.cos(angles), jnp.sin(angles))

def rotate(values, cosine, sine):
    half = values.shape[-1] // 2
    first, second = (values[..., :half], values[..., half:])
    cosine, sine = (cosine[:, None, :], sine[:, None, :])
    return jnp.concatenate([first * cosine - second * sine, second * cosine + first * sine], -1)

def matmul(left, right):
    return jnp.dot(left, right, precision=lax.Precision.HIGHEST)

def block(inputs, w_q, w_o, w_u, w_d, gain_a, gain_m, visible, cosine, sine):
    rows = inputs.shape[0]
    normed = low(normalize(inputs, gain_a))
    projected = matmul(normed, w_q).reshape(rows, HEADS, 3, HEAD_DIM)
    queries = low(rotate(low_back(projected[:, :, 0]), cosine, sine))
    keys = low(rotate(low_back(projected[:, :, 1]), cosine, sine))
    values = low(low_back(projected[:, :, 2]))
    scores = low_back(jnp.einsum('qhd,khd->hqk', queries, keys, precision=lax.Precision.HIGHEST) * HEAD_DIM ** (-0.5))
    scores = jnp.where(visible[None], scores, -1e+30)
    probs = jax.nn.softmax(scores, -1)
    attended = jnp.einsum('hqk,khd->qhd', low(probs), values, precision=lax.Precision.HIGHEST)
    attended = low(low_back(attended.reshape(rows, HEADS * HEAD_DIM)))
    middle = inputs + low_back(matmul(attended, w_o))
    normed_mid = low(normalize(middle, gain_m))
    hidden = low(jax.nn.gelu(low_back(matmul(normed_mid, w_u)), approximate=True))
    return low_back(middle + low_back(matmul(hidden, w_d)))

def layers(current, history, w_q, w_o, w_u, w_d, gain_a, gain_m, first, second, visible, cosine, sine):
    first_out = block(current, w_q[0], w_o[0], w_u[0], w_d[0], gain_a[0], gain_m[0], visible, cosine, sine)
    blended = jnp.einsum('p,ptd->td', first[:PAST], history, precision=lax.Precision.HIGHEST)
    following = low(blended + first[PAST] * first_out)
    second_out = block(following, w_q[1], w_o[1], w_u[1], w_d[1], gain_a[1], gain_m[1], visible, cosine, sine)
    result = jnp.einsum('p,ptd->td', second[:PAST], history, precision=lax.Precision.HIGHEST)
    return result + second[PAST] * first_out + second[PAST + 1] * second_out

def reference(current, history, cotangent, seq_lengths, w_qkv, w_out, w_up, w_down, gain_attn, gain_mlp, dwa_first, dwa_second):
    groups = N_DP
    rows = TOK_DEV
    params = (w_qkv.astype(jnp.float32), w_out.astype(jnp.float32), w_up.astype(jnp.float32), w_down.astype(jnp.float32), gain_attn.astype(jnp.float32), gain_mlp.astype(jnp.float32), dwa_first.astype(jnp.float32), dwa_second.astype(jnp.float32))
    current_rows = current.reshape(groups, rows, D)
    history_rows = history.reshape(PAST, groups, rows, D).transpose(1, 0, 2, 3)
    cotangent_rows = cotangent.reshape(groups, rows, D)

    def step(totals, item):
        cur_row, hist_row, cot_row, lengths = item
        visible, cosine, sine = tables(lengths, rows, HEAD_DIM)

        def forward(inputs, past, *weights):
            return layers(inputs, past, *weights, visible, cosine, sine)
        result, pull = jax.vjp(forward, cur_row.astype(jnp.float32), hist_row.astype(jnp.float32), *params)
        grads = pull(cot_row.astype(jnp.float32))
        totals = tuple((a + b for a, b in zip(totals, grads[2:])))
        return (totals, (result.astype(jnp.bfloat16), grads[0].astype(jnp.bfloat16), grads[1].astype(jnp.bfloat16)))
    start = tuple((jnp.zeros_like(p) for p in params))
    totals, (mixed, grad_cur, grad_hist) = lax.scan(step, start, (current_rows, history_rows, cotangent_rows, seq_lengths))
    mixed = mixed.reshape(groups * rows, D)
    grad_cur = grad_cur.reshape(groups * rows, D)
    grad_hist = grad_hist.transpose(1, 0, 2, 3).reshape(PAST, groups * rows, D)
    return (mixed, grad_cur, grad_hist, totals[0], totals[1], totals[2], totals[3], totals[4], totals[5], totals[6], totals[7])
```

```python
import functools
import types

import jax
import jax.numpy as jnp
import numpy as np
from jax import lax
from jax.experimental import pallas as pl
from jax.experimental.pallas import tpu as pltpu
from jax.sharding import PartitionSpec as P

HEAD = 64
EPS = 1e-05
F32 = jnp.float32
BF16 = jnp.bfloat16
MESH = pl.DeviceIdType.MESH
GELU_A = 0.7978845608
GELU_B = 0.044715
HIDDEN_AXES = (((1,), (0,)), ((), ()))
SHARED_AXES = (((1,), (1,)), ((), ()))
TOKEN_AXES = (((0,), (0,)), ((), ()))

C_N1, C_OUT, C_N2, C_DN, C_GY, C_BP, C_GM, C_NP = 0, 2, 4, 6, 8, 10, 12, 14
C_CUR, C_COT, C_B1, C_MIX, C_GN, C_GC, C_SM, C_ALL = 16, 18, 20, 22, 24, 26, 28, 29
X_H0, X_AR, X_RS, X_GY, X_ARB, X_RSB, X_SM, X_ALL = 0, 2, 4, 6, 8, 10, 12, 13


def nn(a, b):
    return lax.dot_general(a, b, HIDDEN_AXES, preferred_element_type=F32)


def nt(a, b):
    return lax.dot_general(a, b, SHARED_AXES, preferred_element_type=F32)


def tn(a, b):
    return lax.dot_general(a, b, TOKEN_AXES, preferred_element_type=F32)


def center(values):
    shifted = values - jnp.mean(values, -1, keepdims=True)
    scale = lax.rsqrt(jnp.mean(shifted * shifted, -1, keepdims=True) + EPS)
    return shifted * scale, scale


def center_back(e, z, scale):
    return (e - jnp.mean(e, -1, keepdims=True) - z * jnp.mean(e * z, -1, keepdims=True)) * scale


def loop(count, step):
    def one(i, carry):
        step(i)
        return carry

    lax.fori_loop(0, count, one, 0)


def kernel(names, cfg, *refs):
    r = types.SimpleNamespace(**dict(zip(names, refs)))
    rows, width, heads, units, past, inner = cfg
    half, own_width = width // 2, width // 4
    chunk, sub = rows // 2, rows // 4
    block, strip = width // 8, own_width // 4
    count = 2

    m = lax.axis_index("mp")
    core, xx = lax.rem(m, 2), m // 2
    core_peer = {"mp": m + 1 - 2 * core}
    x_peer = {"mp": lax.rem(m + 2, 4)}
    if inner:
        d = lax.axis_index("dp")
        yy, zz = lax.rem(d, 2), d // 2
        y_peer = {"dp": d + 1 - 2 * yy}
        z_peers = [{"dp": lax.rem(d + 2 * step, 8)} for step in (1, 2, 3)]
    own_half = pl.ds(pl.multiple_of(xx * half, 128), half)
    far_half = pl.ds(pl.multiple_of((1 - xx) * half, 128), half)

    def at(k, who):
        return pl.ds(pl.multiple_of(k * chunk + who * sub, 32), sub)

    def of(k):
        return slice(k * chunk, (k + 1) * chunk)

    def mine(k):
        return at(k, core)

    def theirs(k):
        return at(k, 1 - core)

    def over_core(which, src, dst):
        return pltpu.make_async_remote_copy(
            src_ref=src,
            dst_ref=dst,
            send_sem=r.core_send.at[which],
            recv_sem=r.core_recv.at[which],
            device_id=core_peer,
            device_id_type=MESH,
        )

    def over_x(which, src, dst):
        return pltpu.make_async_remote_copy(
            src_ref=src,
            dst_ref=dst,
            send_sem=r.x_send.at[which],
            recv_sem=r.x_recv.at[which],
            device_id=x_peer,
            device_id_type=MESH,
        )

    loads = []
    for index, (src, dst) in enumerate(
        (
            (r.current, r.cur_t),
            (r.cotangent, r.cot_t),
            (r.cos_table, r.cosine),
            (r.sin_table, r.sine),
            (r.w_qkv, r.wq),
            (r.w_out, r.wo),
            (r.w_up, r.wu),
            (r.w_down, r.wd),
        )
    ):
        loads.append(pltpu.make_async_copy(src, dst, r.load_sem.at[index]))
        loads[index].start()

    def history_in(step, slot):
        return pltpu.make_async_copy(
            r.history.at[:, pl.ds(step * strip, strip), :], r.hist.at[slot], r.hist_in.at[slot]
        )

    history_in(0, 0).start()
    history_in(1, 1).start()

    barrier = pltpu.get_barrier_semaphore()
    peers = [core_peer, x_peer] + ([y_peer] + z_peers if inner else [])
    for peer in peers:
        pl.semaphore_signal(barrier, inc=1, device_id=peer, device_id_type=MESH)
    pl.semaphore_wait(barrier, len(peers))

    def c_n1(l, k):
        return over_core(C_N1 + k, r.n1.at[l, mine(k)], r.n1.at[l, mine(k)])

    def c_out(k):
        return over_core(C_OUT + k, r.cstage.at[k], r.crecv_fwd.at[k])

    def c_n2(l, k):
        return over_core(C_N2 + k, r.n2.at[l, mine(k)], r.n2.at[l, mine(k)])

    def c_dn(k):
        return over_core(C_DN + k, r.cstage.at[k], r.crecv_fwd.at[k])

    def c_gy(k):
        return over_core(C_GY + k, r.gy.at[mine(k)], r.gy.at[mine(k)])

    def c_bp(k):
        return over_core(C_BP + k, r.cstage.at[k], r.crecv_bwd.at[k])

    def c_gm(k):
        return over_core(C_GM + k, r.gm.at[mine(k)], r.gm.at[mine(k)])

    def c_np(k):
        return over_core(C_NP + k, r.cstage.at[k], r.crecv_bwd.at[k])

    def c_cur(k):
        return over_core(C_CUR + k, r.cur.at[theirs(k)], r.cv_cur.at[k])

    def c_cot(k):
        return over_core(C_COT + k, r.cot.at[theirs(k)], r.cv_cot.at[k])

    def c_b1(k):
        return over_core(C_B1 + k, r.blend1.at[theirs(k)], r.cv_b1.at[k])

    def c_mix(k):
        return over_core(C_MIX + k, r.cs_mix.at[k], r.cv_mix.at[k])

    def c_gn(k):
        return over_core(C_GN + k, r.cs_gn.at[k], r.cv_gn.at[k])

    def c_gc(k):
        return over_core(C_GC + k, r.cs_gc.at[k], r.cv_gc.at[k])

    def x_h0(l, k):
        return over_x(X_H0 + k, r.xs.at[l, k, :, own_half], r.xs.at[l, k, :, own_half])

    def x_ar(k):
        return over_x(X_AR + k, r.xstage.at[k], r.xrecv_whole.at[k])

    def x_rs(k):
        return over_x(X_RS + k, r.xstage_half.at[k], r.xrecv_half.at[k])

    def x_gy(k):
        return over_x(X_GY + k, r.gy.at[mine(k), own_half], r.gy.at[mine(k), own_half])

    def x_arb(k):
        return over_x(X_ARB + k, r.xstage.at[k], r.xrecv_whole.at[k])

    def x_rsb(k):
        return over_x(X_RSB + k, r.xstage_half.at[k], r.xrecv_half.at[k])

    def to_home(feature, recv, k):
        own, other = feature[mine(k), :].astype(F32), recv[k].astype(F32)
        first = core == 0
        r.home[:, :own_width] = jnp.where(first, own, other)
        r.home[:, own_width:] = jnp.where(first, other, own)
        return r.home[...]

    def from_home(values, keep, stage, k):
        first = core == 0
        low, high = values[:, :own_width], values[:, own_width:]
        keep[mine(k), :] = jnp.where(first, low, high).astype(keep.dtype)
        stage[k] = jnp.where(first, high, low).astype(stage.dtype)

    loads[0].wait()
    r.cur[...] = r.cur_t[...].astype(F32).T.astype(BF16)
    for k in range(count):
        c_cur(k).start()
    loads[1].wait()
    r.cot[...] = r.cot_t[...].astype(F32).T.astype(BF16)
    for k in range(count):
        c_cot(k).start()
    for k in range(count):
        c_cur(k).wait()
        r.xs[0, k, :, own_half] = to_home(r.cur, r.cv_cur, k).astype(BF16)
        x_h0(0, k).start()
    for k in (1, 0):
        c_cot(k).wait()
        home = to_home(r.cot, r.cv_cot, k)
        r.cot_home[k] = home.astype(BF16)
        r.gy[mine(k), own_half] = (r.second[past + 1] * home).astype(BF16)
        x_gy(k).start()

    loads[2].wait()
    loads[3].wait()
    segs = r.seq.shape[1]
    starts, ends = [], []
    total = jnp.int32(0)
    for index in range(segs):
        starts.append(total)
        total = total + r.seq[0, index]
        ends.append(total)
    cos_start = [r.cosine[pl.ds(jnp.clip(s, 0, rows - 1), 1), :] for s in starts]
    sin_start = [r.sine[pl.ds(jnp.clip(s, 0, rows - 1), 1), :] for s in starts]

    def make_tables(i):
        here = pl.ds(pl.multiple_of(i * sub, 32), sub)
        place = lax.broadcasted_iota(jnp.int32, (sub, 128), 0) + i * sub
        lane = lax.broadcasted_iota(jnp.int32, (sub, 128), 1)
        cos_s = jnp.broadcast_to(cos_start[0], (sub, 128))
        sin_s = jnp.broadcast_to(sin_start[0], (sub, 128))
        begin = jnp.zeros((sub, 1), jnp.int32)
        line = lax.broadcasted_iota(jnp.int32, (sub, 1), 0) + i * sub
        for index in range(1, segs):
            inside = place >= ends[index - 1]
            cos_s = jnp.where(inside, cos_start[index], cos_s)
            sin_s = jnp.where(inside, sin_start[index], sin_s)
            begin = jnp.where(line >= ends[index - 1], starts[index], begin)
        cos_t, sin_t = r.cosine[here, :], r.sine[here, :]
        sine = sin_t * cos_s - cos_t * sin_s
        r.rope_cos[here, :] = cos_t * cos_s + sin_t * sin_s
        r.rope_sin[here, :] = jnp.where(lax.rem(lane, HEAD) < HEAD // 2, -sine, sine)
        query = lax.broadcasted_iota(jnp.int32, (sub, rows), 0) + i * sub
        key = lax.broadcasted_iota(jnp.int32, (sub, rows), 1)
        r.bias[here, :] = jnp.where(
            (key <= query) & (key >= begin), 0.0, -1e30
        ).astype(BF16)

    loop(4, make_tables)

    def turn(values, here, sign):
        lane = lax.broadcasted_iota(jnp.int32, values.shape, 1)
        other = jnp.where(
            lax.rem(lane, HEAD) < HEAD // 2,
            pltpu.roll(values, 128 - HEAD // 2, 1),
            pltpu.roll(values, HEAD // 2, 1),
        )
        return values * r.rope_cos[here, :] + sign * (other * r.rope_sin[here, :])

    r.gains[...] = jnp.zeros_like(r.gains)
    r.dots[...] = jnp.zeros_like(r.dots)

    def fold(values):
        return jnp.sum(values, 0, keepdims=True)

    for step in range(4):
        slot = step % 2
        here = slice(step * strip, (step + 1) * strip)
        history_in(step, slot).wait()
        grad = r.cot_t[here, :].astype(F32)
        one = jnp.zeros((strip, rows), F32)
        two = jnp.zeros((strip, rows), F32)
        for j in range(past):
            value = r.hist[slot, j].astype(F32)
            one = one + r.first[j] * value
            two = two + r.second[j] * value
            r.dots[16 + j : 17 + j, :] += fold(value * grad)
        r.blend1_t[here, :] = one
        r.blend2_t[here, :] = two
        if step + 2 < 4:
            history_in(step + 2, slot).start()
    r.blend1[...] = r.blend1_t[...].T
    for k in range(count):
        c_b1(k).start()
    for k in range(count):
        c_b1(k).wait()
        r.blend1_home[k] = to_home(r.blend1, r.cv_b1, k)

    for load in loads[4:]:
        load.wait()

    def norm_in(l, k):
        x_h0(l, k).wait()
        z, scale = center(r.xs[l, k].astype(F32))
        r.z1[l, k] = z.astype(BF16)
        r.s1[l, k] = scale
        r.n1[l, mine(k)] = (z * r.gain_attn[pl.ds(l, 1), :]).astype(BF16)
        c_n1(l, k).start()

    def project(l, k):
        c_n1(l, k).wait()

        here = of(k)
        acc = nt(r.n1[l, here], r.wq[l])
        for h in range(heads):
            base = h * 3 * HEAD
            pair = turn(acc[:, base : base + 2 * HEAD], here, 1.0)
            r.q[l, h, here, :] = (pair[:, :HEAD] * HEAD**-0.5).astype(BF16)
            r.k[l, h, here, :] = pair[:, HEAD:].astype(BF16)
            r.v[l, h, here, :] = acc[:, base + 2 * HEAD : base + 3 * HEAD].astype(BF16)

    def attend(l, k):
        seen = (k + 1) * chunk
        here = of(k)
        for h in range(heads):
            scores = nt(r.q[l, h, here, :], r.k[l, h, :seen, :]) + r.bias[here, :seen].astype(F32)
            top = jnp.max(scores, -1, keepdims=True)
            probs = jnp.exp(scores - top)
            total = jnp.sum(probs, -1, keepdims=True)
            result = nn(probs.astype(BF16), r.v[l, h, :seen, :]) / total
            r.att[l, here, h * HEAD : (h + 1) * HEAD] = result.astype(BF16)
            r.lse[l, here, h : h + 1] = top + jnp.log(total)

    def split_sum(k, total, send):
        for who in (0, 1):

            @pl.when(core == who)
            def _(who=who):
                other = slice((1 - who) * sub, (2 - who) * sub)
                own = slice(who * sub, (who + 1) * sub)
                r.cstage[k] = total[other].astype(BF16)
                send.start()
                r.acc[k] = total[own]

    def project_out(l, k):
        split_sum(k, nn(r.att[l, of(k)], r.wo[l]), c_out(k))

    def chip_sum(k, arrival, received, onward):
        arrival.wait()
        total = r.acc[k] + received[k].astype(F32)
        r.acc[k] = total
        r.xstage[k] = total.astype(BF16)
        onward.start()

    def norm_mid(l, k):
        x_ar(k).wait()
        middle = r.xs[l, k].astype(F32) + r.acc[k] + r.xrecv_whole[k].astype(F32)
        r.mid[k] = middle
        z, scale = center(middle)
        r.z2[l, k] = z.astype(BF16)
        r.s2[l, k] = scale
        r.n2[l, mine(k)] = (z * r.gain_mlp[pl.ds(l, 1), :]).astype(BF16)
        c_n2(l, k).start()

    def feed(l, k):
        c_n2(l, k).wait()

        here = of(k)
        pre = nn(r.n2[l, here], r.wu[l])
        square = pre * pre
        wave = jnp.tanh(pre * (GELU_A + GELU_A * GELU_B * square))
        left = 0.5 + 0.5 * wave
        hidden = (pre * left).astype(BF16)
        slope = left + (0.5 - 0.5 * wave * wave) * pre * (
            GELU_A + 3.0 * GELU_A * GELU_B * square
        )
        r.hid[l, here] = hidden
        r.slope[l, here] = slope.astype(BF16)
        split_sum(k, nn(hidden, r.wd[l]), c_dn(k))

    def chip_scatter(k):
        c_dn(k).wait()
        far = r.acc[k, :, far_half] + r.crecv_fwd[k, :, far_half].astype(F32)
        r.xstage_half[k] = far.astype(BF16)
        x_rs(k).start()

    def block_out(l, k):
        x_rs(k).wait()
        y = (
            r.mid[k, :, own_half]
            + r.acc[k, :, own_half]
            + r.crecv_fwd[k, :, own_half].astype(F32)
            + r.xrecv_half[k].astype(F32)
        )
        grad = r.cot_home[k].astype(F32)

        @pl.when(l == 0)
        def _():
            r.y0[k] = y
            following = r.blend1_home[k] + r.first[past] * y
            r.xs[1, k, :, own_half] = following.astype(BF16)
            x_h0(1, k).start()
            r.dots[16 + past : 17 + past, :half] += fold(y * grad)

        @pl.when(l == 1)
        def _():
            rest = r.second[past] * r.y0[k] + r.second[past + 1] * y
            from_home(rest, r.blend1, r.cs_mix, k)
            c_mix(k).start()
            r.dots[17 + past : 18 + past, :half] += fold(y * grad)

    def forward(l):
        norm_in(l, 0)
        project(l, 0)

        @pl.when(l == 1)
        def _():
            block_out(0, 1)

        attend(l, 0)
        project_out(l, 0)
        norm_in(l, 1)
        chip_sum(0, c_out(0), r.crecv_fwd, x_ar(0))
        project(l, 1)
        attend(l, 1)
        project_out(l, 1)

        @pl.when(l == 0)
        def _():
            for k in (1, 0):
                x_gy(k).wait()
                c_gy(k).start()

        norm_mid(l, 0)
        chip_sum(1, c_out(1), r.crecv_fwd, x_ar(1))
        feed(l, 0)
        chip_scatter(0)
        norm_mid(l, 1)
        feed(l, 1)
        block_out(l, 0)
        chip_scatter(1)


    def feed_back(l, k):

        here = of(k)
        grad = nt(r.gy[here], r.wd[l])
        grad = (grad * r.slope[l, here].astype(F32)).astype(BF16)
        r.gp[here] = grad
        split_sum(k, nt(grad, r.wu[l]), c_bp(k))

    def mid_back(l, k):
        x_arb(k).wait()
        grad = r.acc[k] + r.xrecv_whole[k].astype(F32)
        z = r.z2[l, k].astype(F32)
        gain = r.gain_mlp[pl.ds(l, 1), :]
        once = jnp.where(xx == 0, 1.0, 0.0)
        r.gains[pl.ds(2 + l, 1), :] += once * fold(grad * z)
        total = r.gy[mine(k)].astype(F32) + center_back(grad * gain, z, r.s2[l, k])
        r.mid[k] = total
        r.gm[mine(k)] = total.astype(BF16)
        c_gm(k).start()

    def attend_back(l, k):
        c_gm(k).wait()
        seen = (k + 1) * chunk
        if k == 1:
            r.dqk[...] = jnp.zeros_like(r.dqk)
            r.dv[...] = jnp.zeros_like(r.dv)

        here = of(k)
        grads = nt(r.gm[here], r.wo[l]).astype(BF16)
        for h in range(heads):
            lanes = slice(h * HEAD, (h + 1) * HEAD)
            grad = grads[:, lanes]
            inner_sum = jnp.sum(
                grad.astype(F32) * r.att[l, here, lanes].astype(F32), -1, keepdims=True
            )
            q, keys, vals = r.q[l, h, here, :], r.k[l, h, :seen, :], r.v[l, h, :seen, :]
            scores = nt(q, keys) + r.bias[here, :seen].astype(F32)
            probs = jnp.exp(scores - r.lse[l, here, h : h + 1])
            grad_scores = (probs * (nt(grad, vals) - inner_sum)).astype(BF16)
            r.dqk[h, here, :HEAD] = nn(grad_scores, keys) * HEAD**-0.5
            r.dqk[h, :seen, HEAD:] += tn(grad_scores, q)
            r.dv[:seen, lanes] += tn(probs.astype(BF16), grad)
        for h in range(heads):
            base = h * 3 * HEAD
            pair = turn(r.dqk[h, here, :], here, -1.0)
            r.dqkv[here, base : base + 2 * HEAD] = pair.astype(BF16)
            r.dqkv[here, base + 2 * HEAD : base + 3 * HEAD] = r.dv[here, h * HEAD : (h + 1) * HEAD].astype(BF16)
        split_sum(k, nn(r.dqkv[here], r.wq[l]), c_np(k))

    def in_back(l, k):
        c_np(k).wait()
        grad = r.acc[k] + r.crecv_bwd[k].astype(F32)
        z = r.z1[l, k].astype(F32)
        gain = r.gain_attn[pl.ds(l, 1), :]
        r.gains[pl.ds(l, 1), :] += fold(grad * z)
        r.acc[k] = center_back(grad * gain, z, r.s1[l, k])
        r.xstage_half[k] = r.acc[k, :, far_half].astype(BF16)
        x_rsb(k).start()

    def block_back(l, k):
        x_rsb(k).wait()
        grad = r.mid[k, :, own_half] + r.acc[k, :, own_half] + r.xrecv_half[k].astype(F32)

        @pl.when(l == 1)
        def _():
            before = r.first[past] * grad + r.second[past] * r.cot_home[k].astype(F32)
            r.gy[mine(k), own_half] = before.astype(BF16)
            x_gy(k).start()
            from_home(grad, r.grad_next, r.cs_gn, k)
            c_gn(k).start()
            r.dots[past : past + 1, :half] += fold(r.y0[k] * grad)

        @pl.when(l == 0)
        def _():
            from_home(grad, r.grad_current, r.cs_gc, k)
            c_gc(k).start()

    def keep_grad(piece, columns, values):
        for j in range(8):
            r.grads[piece, j % 2, j // 2, :, columns] = values[j * block : (j + 1) * block].astype(BF16)

    def grads_down(l):
        first = 6 * (1 - l)
        values = tn(r.gy[...], r.hid[l])
        keep_grad(first, slice(None), values[:, :half])
        y_start(first)
        keep_grad(first + 1, slice(None), values[:, half:])
        y_start(first + 1)

    def grads_up(l):
        first = 6 * (1 - l) + 2
        values = tn(r.n2[l], r.gp[...])
        keep_grad(first, slice(None), values[:, :half])
        y_start(first)
        keep_grad(first + 1, slice(None), values[:, half:])
        y_start(first + 1)

    def grads_attend(l):
        first = 6 * (1 - l) + 4
        values = tn(r.n1[l], r.dqkv[...])
        keep_grad(first, slice(None), values[:, :half])
        y_start(first)
        keep_grad(first + 1, slice(0, own_width), values[:, half:])
        keep_grad(first + 1, slice(own_width, half), tn(r.gm[...], r.att[l]))
        y_start(first + 1)

    def y_copy(piece):
        return pltpu.make_async_remote_copy(
            src_ref=r.grads.at[piece, 1 - yy],
            dst_ref=r.y_in.at[piece],
            send_sem=r.y_send.at[piece],
            recv_sem=r.y_recv.at[piece],
            device_id=y_peer,
            device_id_type=MESH,
        )

    def z_copy(piece, step):
        return pltpu.make_async_remote_copy(
            src_ref=r.grads.at[piece, yy, lax.rem(zz + step, 4)],
            dst_ref=r.z_in.at[piece, step - 1],
            send_sem=r.z_send.at[piece, step - 1],
            recv_sem=r.z_recv.at[piece, step - 1],
            device_id=z_peers[step - 1],
            device_id_type=MESH,
        )

    def y_start(piece):
        if inner:
            y_copy(piece).start()

    def z_start(piece):
        if not inner:
            return
        y_copy(piece).wait()
        for z in range(4):
            both = r.grads[piece, yy, z].astype(F32) + r.y_in[piece, z].astype(F32)
            r.grads[piece, yy, z] = both.astype(BF16)
        for step in (2, 1, 3):
            z_copy(piece, step).start()

    def z_finish(piece):
        if not inner:
            return
        total = r.grads[piece, yy, zz].astype(F32)
        for step in (1, 2, 3):
            z_copy(piece, step).wait()
            total = total + r.z_in[piece, step - 1].astype(F32)
        r.parts[piece] = total

    loop(2, forward)
    for k in (1, 0):
        c_gy(k).wait()
    grads_down(1)
    block_out(1, 1)

    def backward(i):
        l = 1 - i

        @pl.when(l == 0)
        def _():
            x_gy(1).wait()
            c_gy(1).start()
            z_start(3)
            c_gy(1).wait()

        feed_back(l, 1)

        @pl.when(l == 0)
        def _():
            x_gy(0).wait()
            c_gy(0).start()

        chip_sum(1, c_bp(1), r.crecv_bwd, x_arb(1))

        @pl.when(l == 0)
        def _():
            c_gy(0).wait()

        feed_back(l, 0)

        @pl.when(l == 0)
        def _():
            grads_down(0)

        chip_sum(0, c_bp(0), r.crecv_bwd, x_arb(0))
        grads_up(l)

        @pl.when(l == 0)
        def _():
            z_start(4)

        mid_back(l, 1)

        @pl.when(l == 1)
        def _():
            z_start(0)

        attend_back(l, 1)
        mid_back(l, 0)

        @pl.when(l == 1)
        def _():
            z_start(1)

        @pl.when(l == 0)
        def _():
            z_start(5)

        in_back(l, 1)
        attend_back(l, 0)

        @pl.when(l == 1)
        def _():
            z_start(2)

        block_back(l, 1)

        @pl.when(l == 0)
        def _():
            z_start(6)

        in_back(l, 0)
        grads_attend(l)
        block_back(l, 0)

    loop(2, backward)

    for k in range(count):
        c_mix(k).wait()
        r.blend1[theirs(k), :] = r.cv_mix[k]
        c_gn(k).wait()
        r.grad_next[theirs(k), :] = r.cv_gn[k]
    r.mixed_t[...] = (r.blend2_t[...] + r.blend1[...].T).astype(BF16)
    r.grad_next_t[...] = r.grad_next[...].T

    z_start(7)
    for piece in range(5):
        z_finish(piece)

    history_in(0, 0).start()
    history_in(1, 1).start()
    for step in range(4):
        slot = step % 2
        here = slice(step * strip, (step + 1) * strip)
        history_in(step, slot).wait()
        grad_next = r.grad_next_t[here, :]
        for j in range(past):
            r.dots[j : j + 1, :] += fold(r.hist[slot, j].astype(F32) * grad_next)
        if step in (1, 3):
            z_start(8 + step // 2)
        if step + 2 < 4:
            history_in(step + 2, slot).start()

    z_finish(5)
    z_finish(6)

    small = r.small
    for i in range(width // 128):
        small[0, 4 * i : 4 * i + 4, :] = r.gains[:4, i * 128 : (i + 1) * 128]
    base = width // 32
    small[0, base : base + 32, :] = jnp.broadcast_to(
        jnp.sum(r.dots[...], -1, keepdims=True), (32, 128)
    )
    if inner:
        sm = over_core(C_SM, small.at[0], r.small_in.at[0])
        sm.start()
        sm.wait()
        small[1] = small[0] + r.small_in[0]
        sm = over_x(X_SM, small.at[1], r.small_in.at[1])
        sm.start()
        sm.wait()
        small[2] = small[1] + r.small_in[1]
        sm = pltpu.make_async_remote_copy(
            src_ref=small.at[2],
            dst_ref=r.small_in.at[2],
            send_sem=r.sm_send.at[0],
            recv_sem=r.sm_recv.at[0],
            device_id=y_peer,
            device_id_type=MESH,
        )
        sm.start()
        sm.wait()
        both = small[2] + r.small_in[2]
        small[3] = both
        sends = []
        for step in (1, 2, 3):
            sends.append(
                pltpu.make_async_remote_copy(
                    src_ref=small.at[3],
                    dst_ref=r.small_in.at[2 + step],
                    send_sem=r.sm_send.at[step],
                    recv_sem=r.sm_recv.at[step],
                    device_id=z_peers[step - 1],
                    device_id_type=MESH,
                )
            )
        for send in sends:
            send.start()
        for send in sends:
            send.wait()
        by_z = []
        for z in range(4):
            value = both
            for step in (1, 2, 3):
                value = jnp.where(lax.rem(z + step, 4) == zz, r.small_in[2 + step], value)
            by_z.append(value)
        r.sums[...] = (by_z[0] + by_z[1]) + (by_z[2] + by_z[3])
    else:
        r.sums[...] = small[0]

    for k in range(count):
        c_gc(k).wait()
        r.grad_current[theirs(k), :] = r.cv_gc[k].astype(F32)
    r.grad_current_t[...] = r.grad_current[...].T.astype(BF16)
    z_start(10)
    z_finish(7)
    z_finish(8)
    z_start(11)
    for piece in (9, 10, 11):
        z_finish(piece)
    if not inner:
        out = pltpu.make_async_copy(r.grads, r.raw, r.load_sem.at[0])
        out.start()
        out.wait()


def finish(names, past, *refs):
    r = types.SimpleNamespace(**dict(zip(names, refs)))
    grad, grad_next = r.cotangent[...].astype(F32), r.grad_next_t[...]
    for j in range(past):
        r.grad_history[j] = (r.first[j] * grad_next + r.second[j] * grad).astype(BF16)
    r.mixed[...] = r.mixed_t[...]
    r.grad_current[...] = r.grad_current_t[...]
    width = r.grad_gain_attn.shape[1]
    for i in range(width // 128):
        lanes = slice(i * 128, (i + 1) * 128)
        r.grad_gain_attn[:, lanes] = r.sums[4 * i : 4 * i + 2, :]
        r.grad_gain_mlp[:, lanes] = r.sums[4 * i + 2 : 4 * i + 4, :]
    base = width // 32
    dots = r.sums[base : base + 32, :]
    for j in range(past + 1):
        r.grad_first[j] = dots[j, 0]
    for j in range(past + 2):
        r.grad_second[j] = dots[16 + j, 0]
    half, own_width = width // 2, width // 4
    for l in (0, 1):
        first = 6 * (1 - l)
        for i in (0, 1):
            lanes = slice(i * half, (i + 1) * half)
            r.grad_down[l, :, lanes] = r.parts[first + i]
            r.grad_up[l, :, lanes] = r.parts[first + 2 + i]
        r.grad_qkv[l, :, :half] = r.parts[first + 4]
        r.grad_qkv[l, :, half:] = r.parts[first + 5, :, :own_width]
        r.grad_out[l] = r.parts[first + 5, :, own_width:].T


def tables(rows):
    freqs = 10000.0 ** (-2.0 * np.arange(HEAD // 2) / HEAD)
    angles = np.arange(rows)[:, None] * np.tile(freqs, 4)[None, :]
    return np.cos(angles).astype(np.float32), np.sin(angles).astype(np.float32)


def shards(
    n_dp,
    current,
    history,
    cotangent,
    seq_lengths,
    w_qkv,
    w_out,
    w_up,
    w_down,
    gain_attn,
    gain_mlp,
    dwa_first,
    dwa_second,
):
    rows, own_width = current.shape
    past = history.shape[0]
    layers, width, _ = w_qkv.shape
    heads = w_out.shape[1] // HEAD
    units = w_up.shape[2]
    sub, half, block = rows // 4, width // 2, width // 8
    inner = n_dp == 8
    cos_table, sin_table = tables(rows)

    hbm = pl.BlockSpec(memory_space=pl.ANY)
    vmem = pl.BlockSpec(memory_space=pltpu.VMEM)
    smem = pl.BlockSpec(memory_space=pltpu.SMEM)
    inputs = dict(
        current=(current.T, hbm),
        history=(history.transpose(0, 2, 1), hbm),
        cotangent=(cotangent.T, hbm),
        seq=(seq_lengths, smem),
        w_qkv=(w_qkv.transpose(0, 2, 1), hbm),
        w_out=(w_out, hbm),
        w_up=(w_up, hbm),
        w_down=(w_down, hbm),
        gain_attn=(gain_attn, vmem),
        gain_mlp=(gain_mlp, vmem),
        first=(dwa_first, smem),
        second=(dwa_second, smem),
        cos_table=(jnp.asarray(cos_table), hbm),
        sin_table=(jnp.asarray(sin_table), hbm),
    )

    def shape(dims, kind):
        return jax.ShapeDtypeStruct(dims, kind)

    small_rows = width // 32 + 32
    outputs = dict(
        mixed_t=(shape((own_width, rows), BF16), vmem),
        grad_current_t=(shape((own_width, rows), BF16), vmem),
        grad_next_t=(shape((own_width, rows), F32), vmem),
        sums=(shape((small_rows, 128), F32), vmem),
    )
    if inner:
        outputs.update(
            parts=(shape((6 * layers, block, half), F32), vmem),
        )
    else:
        outputs.update(
            raw=(shape((6 * layers, 2, 4, block, half), BF16), hbm),
        )

    def whole(kind=BF16, *lead):
        return pltpu.VMEM((*lead, rows, width), kind)

    def quarter(kind, *lead):
        return pltpu.VMEM((*lead, sub, width), kind)

    def quarter_half(kind, *lead):
        return pltpu.VMEM((*lead, sub, half), kind)

    def quarter_own(kind, *lead):
        return pltpu.VMEM((*lead, sub, own_width), kind)

    dma = pltpu.SemaphoreType.DMA
    scratch = dict(
        cur=pltpu.VMEM((rows, own_width), BF16),
        cot=pltpu.VMEM((rows, own_width), BF16),
        cosine=pltpu.VMEM((rows, 128), F32),
        sine=pltpu.VMEM((rows, 128), F32),
        rope_cos=pltpu.VMEM((rows, 128), F32),
        rope_sin=pltpu.VMEM((rows, 128), F32),
        bias=pltpu.VMEM((rows, rows), BF16),
        wq=pltpu.VMEM((layers, 3 * own_width, width), BF16),
        wo=pltpu.VMEM(w_out.shape, BF16),
        wu=pltpu.VMEM(w_up.shape, BF16),
        wd=pltpu.VMEM(w_down.shape, BF16),
        cur_t=pltpu.VMEM((own_width, rows), BF16),
        cot_t=pltpu.VMEM((own_width, rows), BF16),
        hist=pltpu.VMEM((2, past, own_width // 4, rows), BF16),
        blend1=pltpu.VMEM((rows, own_width), F32),
        blend1_t=pltpu.VMEM((own_width, rows), F32),
        blend2_t=pltpu.VMEM((own_width, rows), F32),
        grad_current=pltpu.VMEM((rows, own_width), F32),
        grad_next=pltpu.VMEM((rows, own_width), F32),
        blend1_home=quarter_half(F32, 2),
        home=quarter_half(F32),
        cot_home=quarter_half(BF16, 2),
        y0=quarter_half(F32, 2),
        xs=quarter(BF16, layers, 2),
        z1=quarter(BF16, layers, 2),
        z2=quarter(BF16, layers, 2),
        s1=pltpu.VMEM((layers, 2, sub, 1), F32),
        s2=pltpu.VMEM((layers, 2, sub, 1), F32),
        acc=quarter(F32, 2),
        mid=quarter(F32, 2),
        n1=whole(BF16, layers),
        n2=whole(BF16, layers),
        hid=pltpu.VMEM((layers, rows, units), BF16),
        slope=pltpu.VMEM((layers, rows, units), BF16),
        gp=pltpu.VMEM((rows, units), BF16),
        gy=whole(),
        gm=whole(),
        q=pltpu.VMEM((layers, heads, rows, HEAD), BF16),
        k=pltpu.VMEM((layers, heads, rows, HEAD), BF16),
        v=pltpu.VMEM((layers, heads, rows, HEAD), BF16),
        att=pltpu.VMEM((layers, rows, own_width), BF16),
        lse=pltpu.VMEM((layers, rows, heads), F32),
        dqk=pltpu.VMEM((heads, rows, 2 * HEAD), F32),
        dv=pltpu.VMEM((rows, own_width), F32),
        dqkv=pltpu.VMEM((rows, 3 * own_width), BF16),
        gains=pltpu.VMEM((8, width), F32),
        dots=pltpu.VMEM((32, rows), F32),
        small=pltpu.VMEM((4, small_rows, 128), F32),
        small_in=pltpu.VMEM((6, small_rows, 128), F32),
        cstage=quarter(BF16, 2),
        crecv_fwd=quarter(BF16, 2),
        crecv_bwd=quarter(BF16, 2),
        xstage=quarter(BF16, 2),
        xrecv_whole=quarter(BF16, 2),
        xstage_half=quarter_half(BF16, 2),
        xrecv_half=quarter_half(BF16, 2),
        cv_cur=quarter_own(BF16, 2),
        cv_cot=quarter_own(BF16, 2),
        cv_b1=quarter_own(F32, 2),
        cs_mix=quarter_own(F32, 2),
        cv_mix=quarter_own(F32, 2),
        cs_gn=quarter_own(F32, 2),
        cv_gn=quarter_own(F32, 2),
        cs_gc=quarter_own(BF16, 2),
        cv_gc=quarter_own(BF16, 2),
        grads=pltpu.VMEM((6 * layers, 2, 4, block, half), BF16),
        load_sem=dma((8,)),
        hist_in=dma((2,)),
        hist_out=dma((2,)),
        core_send=dma((C_ALL,)),
        core_recv=dma((C_ALL,)),
        x_send=dma((X_ALL,)),
        x_recv=dma((X_ALL,)),
    )
    if inner:
        scratch.update(
            y_in=pltpu.VMEM((6 * layers, 4, block, half), BF16),
            z_in=pltpu.VMEM((6 * layers, 3, block, half), BF16),
            y_send=dma((6 * layers,)),
            y_recv=dma((6 * layers,)),
            z_send=dma((6 * layers, 3)),
            z_recv=dma((6 * layers, 3)),
            sm_send=dma((4,)),
            sm_recv=dma((4,)),
        )
    names = [*inputs, *outputs, *scratch]
    results = pl.pallas_call(
        functools.partial(kernel, names, (rows, width, heads, units, past, inner)),
        out_shape=[o[0] for o in outputs.values()],
        in_specs=[i[1] for i in inputs.values()],
        out_specs=[o[1] for o in outputs.values()],
        scratch_shapes=[*scratch.values()],
        compiler_params=pltpu.CompilerParams(
            collective_id=0, has_side_effects=True, vmem_limit_bytes=63 * 2**20
        ),
    )(*[i[0] for i in inputs.values()])
    out = types.SimpleNamespace(**dict(zip(outputs, results)))
    if not inner:
        out.sums = lax.psum(out.sums, ("dp", "mp"))

        raw = out.raw.transpose(0, 2, 1, 3, 4).reshape(6 * layers, width, half).astype(F32)
        out.parts = lax.psum_scatter(raw, "dp", scatter_dimension=1, tiled=True)
    share = out.parts.shape[1]
    given = dict(
        cotangent=(cotangent.T, vmem),
        first=(dwa_first, smem),
        second=(dwa_second, smem),
        mixed_t=(out.mixed_t, vmem),
        grad_current_t=(out.grad_current_t, vmem),
        grad_next_t=(out.grad_next_t, vmem),
        sums=(out.sums, vmem),
        parts=(out.parts, vmem),
    )
    wanted = dict(
        mixed=(shape((own_width, rows), BF16), vmem),
        grad_current=(shape((own_width, rows), BF16), vmem),
        grad_history=(shape((past, own_width, rows), BF16), vmem),
        grad_qkv=(shape((layers, share, 3 * own_width), F32), vmem),
        grad_out=(shape((layers, own_width, share), F32), vmem),
        grad_up=(shape((layers, share, units), F32), vmem),
        grad_down=(shape((layers, share, units), F32), vmem),
        grad_gain_attn=(shape((layers, width), F32), vmem),
        grad_gain_mlp=(shape((layers, width), F32), vmem),
        grad_first=(shape((past + 1,), F32), smem),
        grad_second=(shape((past + 2,), F32), smem),
    )
    results = pl.pallas_call(
        functools.partial(finish, [*given, *wanted], past),
        out_shape=[o[0] for o in wanted.values()],
        in_specs=[i[1] for i in given.values()],
        out_specs=[o[1] for o in wanted.values()],
        compiler_params=pltpu.CompilerParams(vmem_limit_bytes=62 * 2**20),
    )(*[i[0] for i in given.values()])
    out = types.SimpleNamespace(**dict(zip(wanted, results)))
    return (
        out.mixed.T,
        out.grad_current.T,
        out.grad_history.transpose(0, 2, 1),
        out.grad_qkv,
        out.grad_out,
        out.grad_up,
        out.grad_down.transpose(0, 2, 1),
        out.grad_gain_attn,
        out.grad_gain_mlp,
        out.grad_first,
        out.grad_second,
    )


def solution(mesh):
    in_specs = (
        P("dp", "mp"),
        P(None, "dp", "mp"),
        P("dp", "mp"),
        P("dp", None),
        P(None, None, "mp"),
        P(None, "mp", None),
        P(None, None, "mp"),
        P(None, "mp", None),
        P(),
        P(),
        P(),
        P(),
    )
    out_specs = (
        P("dp", "mp"),
        P("dp", "mp"),
        P(None, "dp", "mp"),
        P(None, "dp", "mp"),
        P(None, "mp", "dp"),
        P(None, "dp", "mp"),
        P(None, "mp", "dp"),
        P(),
        P(),
        P(),
        P(),
    )
    return jax.shard_map(
        functools.partial(shards, mesh.shape["dp"]),
        mesh=mesh,
        in_specs=in_specs,
        out_specs=out_specs,
        check_vma=False,
    )
```

```python
import functools
import types

import jax
import jax.numpy as jnp
import numpy as np
from jax import lax
from jax.experimental import pallas as pl
from jax.experimental.pallas import tpu as pltpu
from jax.sharding import PartitionSpec as P

HEAD = 64
EPS = 1e-05
F32 = jnp.float32
BF16 = jnp.bfloat16
MESH = pl.DeviceIdType.MESH
CHUNKS = 4
GELU_A = 0.7978845608
GELU_B = 0.044715
HIDDEN_AXES = (((1,), (0,)), ((), ()))
SHARED_AXES = (((1,), (1,)), ((), ()))
TOKEN_AXES = (((0,), (0,)), ((), ()))

def nn(a, b):
    return lax.dot_general(a, b, HIDDEN_AXES, preferred_element_type=F32)


def nt(a, b):
    return lax.dot_general(a, b, SHARED_AXES, preferred_element_type=F32)


def tn(a, b):
    return lax.dot_general(a, b, TOKEN_AXES, preferred_element_type=F32)


def center(values):
    shifted = values - jnp.mean(values, -1, keepdims=True)
    scale = lax.rsqrt(jnp.mean(shifted * shifted, -1, keepdims=True) + EPS)
    return shifted * scale, scale


def center_back(e, z, scale):
    return (e - jnp.mean(e, -1, keepdims=True) - z * jnp.mean(e * z, -1, keepdims=True)) * scale


def kernel(names, cfg, *refs):
    r = types.SimpleNamespace(**dict(zip(names, refs)))
    rows, width, heads, units, past, count, inner = cfg
    half, own_width = width // 2, width // 4
    chunk, sub = rows // count, rows // (2 * count)
    block, strip = width // 8, own_width // 4
    chunks = range(count)

    m = lax.axis_index("mp")
    core, xx = lax.rem(m, 2), m // 2
    core_peer = {"mp": m + 1 - 2 * core}
    x_peer = {"mp": lax.rem(m + 2, 4)}
    y_peer, z_peers = None, []
    if inner:
        d = lax.axis_index("dp")
        yy, zz = lax.rem(d, 2), d // 2
        y_peer = {"dp": d + 1 - 2 * yy}
        z_peers = [{"dp": lax.rem(d + 2 * step, 8)} for step in (1, 2, 3)]
    own_half = pl.ds(pl.multiple_of(xx * half, 128), half)
    far_half = pl.ds(pl.multiple_of((1 - xx) * half, 128), half)

    def of(k):
        return slice(k * chunk, (k + 1) * chunk)

    def mine(k):
        return pl.ds(pl.multiple_of(k * chunk + core * sub, 16), sub)

    def theirs(k):
        return pl.ds(pl.multiple_of(k * chunk + (1 - core) * sub, 16), sub)

    loads = []
    for index, (src, dst) in enumerate(
        (
            (r.current, r.cur_t),
            (r.cotangent, r.cot_t),
            (r.cos_table, r.rope_cos),
            (r.sin_table, r.rope_sin),
            (r.w_qkv, r.wq),
            (r.w_out, r.wo),
            (r.w_up, r.wu),
            (r.w_down, r.wd),
        )
    ):
        loads.append(pltpu.make_async_copy(src, dst, r.load_sem.at[index]))
    for index in (0, 2, 3, 1):
        loads[index].start()
    history = []
    for step in range(4):
        here = slice(step * strip, (step + 1) * strip)
        history.append(
            pltpu.make_async_copy(
                r.history.at[:, here, :], r.hist.at[:, here, :], r.hist_in.at[step]
            )
        )
        history[step].start()
    for load in loads[4:]:
        load.start()

    barrier = pltpu.get_barrier_semaphore()
    peers = [core_peer, x_peer] + ([y_peer] + z_peers if inner else [])
    for peer in peers:
        pl.semaphore_signal(barrier, inc=1, device_id=peer, device_id_type=MESH)
    pl.semaphore_wait(barrier, len(peers))

    def remote(src, dst, send, recv, peer):
        return pltpu.make_async_remote_copy(
            src_ref=src,
            dst_ref=dst,
            send_sem=send,
            recv_sem=recv,
            device_id=peer,
            device_id_type=MESH,
        )

    def over_core(kind, k, src, dst):
        return remote(src, dst, r.core_send.at[kind, k], r.core_recv.at[kind, k], core_peer)

    def over_x(kind, k, src, dst):
        return remote(src, dst, r.x_send.at[kind, k], r.x_recv.at[kind, k], x_peer)

    def c_cur(k):
        return over_core(0, k, r.cur.at[theirs(k)], r.cv_cur.at[k])

    def c_cot(k):
        return over_core(1, k, r.cot.at[theirs(k)], r.cv_cot.at[k])

    def c_b1(k):
        return over_core(2, k, r.blend1.at[theirs(k)], r.cv_wide.at[k])

    def c_n1(l, k):
        return over_core(3, k, r.n1.at[l, mine(k)], r.n1.at[l, mine(k)])

    def c_out(k):
        return over_core(4, k, r.cstage.at[k], r.crecv_fwd.at[k])

    def c_n2(l, k):
        return over_core(5, k, r.n2.at[l, mine(k)], r.n2.at[l, mine(k)])

    def c_dn(k):
        return over_core(6, k, r.cstage.at[k], r.crecv_fwd.at[k])

    def c_mix(k):
        return over_core(7, k, r.cs_wide.at[k], r.cv_wide.at[k])

    def c_gy(k):
        return over_core(8, k, r.gy.at[mine(k)], r.gy.at[mine(k)])

    def c_bp(k):
        return over_core(9, k, r.cstage.at[k], r.crecv_bwd.at[k])

    def c_gm(k):
        return over_core(10, k, r.gm.at[mine(k)], r.gm.at[mine(k)])

    def c_np(k):
        return over_core(11, k, r.cstage.at[k], r.crecv_bwd.at[k])

    def c_gn(k):
        return over_core(12, k, r.cs_wide.at[k], r.cv_wide.at[k])

    def c_gc(k):
        return over_core(13, k, r.cs_gc.at[k], r.cv_gc.at[k])

    def x_h0(l, k):
        return over_x(0, k, r.xs.at[l, k, :, own_half], r.xs.at[l, k, :, own_half])

    def x_ar(k):
        return over_x(1, k, r.xstage.at[k], r.xrecv_whole.at[k])

    def x_rs(k):
        return over_x(2, k, r.xstage_half.at[k], r.xrecv_half.at[k])

    def x_gy(k):
        return over_x(3, k, r.gy.at[mine(k), own_half], r.gy.at[mine(k), own_half])

    def x_arb(k):
        return over_x(4, k, r.xstage.at[k], r.xrecv_whole.at[k])

    def x_rsb(k):
        return over_x(5, k, r.xstage_half.at[k], r.xrecv_half.at[k])

    def y_copy(piece):
        return remote(
            r.grads.at[piece, 1 - yy],
            r.y_in.at[piece],
            r.y_send.at[piece],
            r.y_recv.at[piece],
            y_peer,
        )

    def z_copy(piece, step):
        return remote(
            r.grads.at[piece, yy, lax.rem(zz + step, 4)],
            r.z_in.at[piece, step - 1],
            r.z_send.at[piece, step - 1],
            r.z_recv.at[piece, step - 1],
            z_peers[step - 1],
        )

    def sm_copy(stage, slot, peer):
        return remote(
            r.small.at[stage], r.small_in.at[slot], r.sm_send.at[slot], r.sm_recv.at[slot], peer
        )

    def to_home(feature, recv, k):
        own, other = feature[mine(k), :].astype(F32), recv[k].astype(F32)
        first = core == 0
        r.home[:, :own_width] = jnp.where(first, own, other)
        r.home[:, own_width:] = jnp.where(first, other, own)
        return r.home[...]

    def from_home(values, keep, stage, k):
        first = core == 0
        low, high = values[:, :own_width], values[:, own_width:]
        keep[mine(k), :] = jnp.where(first, low, high).astype(keep.dtype)
        stage[k] = jnp.where(first, high, low).astype(stage.dtype)

    def of_chip(values):
        return jnp.where(xx == 0, values[:, :half], values[:, half:])

    def fold(values):
        return jnp.sum(values, 0, keepdims=True)

    def cur():
        loads[0].wait()
        r.cur[...] = r.cur_t[...].astype(F32).T.astype(BF16)
        for k in chunks:
            c_cur(k).start()

    def cot():
        loads[1].wait()
        r.cot[...] = r.cot_t[...].astype(F32).T.astype(BF16)
        for k in reversed(chunks):
            c_cot(k).start()
        r.gains[...] = jnp.zeros_like(r.gains)
        r.dots[...] = jnp.zeros_like(r.dots)

    def cur_home(k):
        c_cur(k).wait()
        r.xs[0, k, :, own_half] = to_home(r.cur, r.cv_cur, k).astype(BF16)
        x_h0(0, k).start()

    def cot_home(k):
        c_cot(k).wait()
        home = to_home(r.cot, r.cv_cot, k)
        r.cot_home[k] = home.astype(BF16)
        r.gy[mine(k), own_half] = (r.second[past + 1] * home).astype(BF16)
        x_gy(k).start()

    def turn_tables():
        loads[2].wait()
        loads[3].wait()
        segs = r.seq.shape[1]
        starts, ends = [], []
        total = jnp.int32(0)
        for index in range(segs):
            starts.append(total)
            total = total + r.seq[0, index]
            ends.append(total)
        cos_start = [r.rope_cos[pl.ds(jnp.clip(s, 0, rows - 1), 1), :] for s in starts]
        sin_start = [r.rope_sin[pl.ds(jnp.clip(s, 0, rows - 1), 1), :] for s in starts]
        size = rows // 4
        for i in range(4):
            here = slice(i * size, (i + 1) * size)
            place = lax.broadcasted_iota(jnp.int32, (size, 128), 0) + i * size
            lane = lax.broadcasted_iota(jnp.int32, (size, 128), 1)
            line = lax.broadcasted_iota(jnp.int32, (size, 1), 0) + i * size
            cos_s = jnp.broadcast_to(cos_start[0], (size, 128))
            sin_s = jnp.broadcast_to(sin_start[0], (size, 128))
            begin = jnp.zeros((size, 1), jnp.int32)
            for index in range(1, segs):
                inside = place >= ends[index - 1]
                cos_s = jnp.where(inside, cos_start[index], cos_s)
                sin_s = jnp.where(inside, sin_start[index], sin_s)
                begin = jnp.where(line >= ends[index - 1], starts[index], begin)
            cos_t, sin_t = r.rope_cos[here, :], r.rope_sin[here, :]
            sine = sin_t * cos_s - cos_t * sin_s
            r.rope_cos[here, :] = cos_t * cos_s + sin_t * sin_s
            r.rope_sin[here, :] = jnp.where(lax.rem(lane, HEAD) < HEAD // 2, -sine, sine)
            query = lax.broadcasted_iota(jnp.int32, (size, rows), 0) + i * size
            key = lax.broadcasted_iota(jnp.int32, (size, rows), 1)
            r.bias[here, :] = jnp.where((key <= query) & (key >= begin), 0.0, -1e30).astype(BF16)

    def turn(values, here, sign):
        lane = lax.broadcasted_iota(jnp.int32, values.shape, 1)
        other = jnp.where(
            lax.rem(lane, HEAD) < HEAD // 2,
            pltpu.roll(values, 128 - HEAD // 2, 1),
            pltpu.roll(values, HEAD // 2, 1),
        )
        return values * r.rope_cos[here, :] + sign * (other * r.rope_sin[here, :])

    def blends(step):
        here = slice(step * strip, (step + 1) * strip)
        history[step].wait()
        grad = r.cot_t[here, :].astype(F32)
        one = jnp.zeros((strip, rows), F32)
        two = jnp.zeros((strip, rows), F32)
        for j in range(past):
            value = r.hist[j, here, :].astype(F32)
            one = one + r.first[j] * value
            two = two + r.second[j] * value
            r.dots[16 + j : 17 + j, :] += fold(value * grad)
        r.grad_next_t[here, :] = one
        r.blend2_t[here, :] = two

    def blend_send():
        r.blend1[...] = r.grad_next_t[...].T
        for k in chunks:
            c_b1(k).start()

    def blend_home(k):
        c_b1(k).wait()
        r.blend1_home[k] = to_home(r.blend1, r.cv_wide, k)

    def norm_in(l, k):
        x_h0(l, k).wait()
        z, scale = center(r.xs[l, k].astype(F32))
        r.z1[l, k] = z.astype(BF16)
        r.s1[l, k] = scale
        r.n1[l, mine(k)] = (z * r.gain_attn[l : l + 1, :]).astype(BF16)
        c_n1(l, k).start()

    def project(l, k):
        if (l, k) == (0, 0):
            for load in loads[4:]:
                load.wait()
        c_n1(l, k).wait()
        here = of(k)
        acc = nt(r.n1[l, here], r.wq[l])
        for h in range(heads):
            base = h * 3 * HEAD
            pair = turn(acc[:, base : base + 2 * HEAD], here, 1.0)
            r.q[l, h, here, :] = (pair[:, :HEAD] * HEAD**-0.5).astype(BF16)
            r.k[l, h, here, :] = pair[:, HEAD:].astype(BF16)
            r.v[l, h, here, :] = acc[:, base + 2 * HEAD : base + 3 * HEAD].astype(BF16)

    def attend(l, k, h):
        seen = (k + 1) * chunk
        here = of(k)
        scores = nt(r.q[l, h, here, :], r.k[l, h, :seen, :]) + r.bias[here, :seen].astype(F32)
        top = jnp.max(scores, -1, keepdims=True)
        probs = jnp.exp(scores - top)
        total = jnp.sum(probs, -1, keepdims=True)
        result = nn(probs.astype(BF16), r.v[l, h, :seen, :]) / total
        r.att[l, here, h * HEAD : (h + 1) * HEAD] = result.astype(BF16)
        r.lse[l, here, h : h + 1] = top + jnp.log(total)

    def split_sum(k, total, send):
        for who in (0, 1):

            @pl.when(core == who)
            def _(who=who):
                other = slice((1 - who) * sub, (2 - who) * sub)
                own = slice(who * sub, (who + 1) * sub)
                r.cstage[k] = total[other].astype(BF16)
                send.start()
                r.acc[k] = total[own]

    def chip_sum(k, arrival, received, onward):
        arrival.wait()
        total = r.acc[k] + received[k].astype(F32)
        r.acc[k] = total
        r.xstage[k] = total.astype(BF16)
        onward.start()

    def project_out(l, k):
        split_sum(k, nn(r.att[l, of(k)], r.wo[l]), c_out(k))

    def out_sum(l, k):
        chip_sum(k, c_out(k), r.crecv_fwd, x_ar(k))

    def norm_mid(l, k):
        x_ar(k).wait()
        middle = r.xs[l, k].astype(F32) + r.acc[k] + r.xrecv_whole[k].astype(F32)
        r.mid[k] = of_chip(middle)
        z, scale = center(middle)
        r.z2[l, k] = z.astype(BF16)
        r.s2[l, k] = scale
        r.n2[l, mine(k)] = (z * r.gain_mlp[l : l + 1, :]).astype(BF16)
        c_n2(l, k).start()

    def feed(l, k):
        c_n2(l, k).wait()
        here = of(k)
        pre = nn(r.n2[l, here], r.wu[l])
        square = pre * pre
        wave = jnp.tanh(pre * (GELU_A + GELU_A * GELU_B * square))
        left = 0.5 + 0.5 * wave
        hidden = (pre * left).astype(BF16)
        slope = left + (0.5 - 0.5 * wave * wave) * pre * (
            GELU_A + 3.0 * GELU_A * GELU_B * square
        )
        r.hid[l, here] = hidden
        r.slope[l, here] = slope.astype(BF16)
        split_sum(k, nn(hidden, r.wd[l]), c_dn(k))

    def chip_scatter(l, k):
        c_dn(k).wait()
        far = r.acc[k, :, far_half] + r.crecv_fwd[k, :, far_half].astype(F32)
        r.xstage_half[k] = far.astype(BF16)
        x_rs(k).start()

    def block_out(l, k):
        x_rs(k).wait()
        y = (
            r.mid[k]
            + r.acc[k, :, own_half]
            + r.crecv_fwd[k, :, own_half].astype(F32)
            + r.xrecv_half[k].astype(F32)
        )
        line = 16 + past + l
        r.dots[line : line + 1, :half] += fold(y * r.cot_home[k].astype(F32))
        if l == 0:
            r.y0[k] = y
            following = r.blend1_home[k] + r.first[past] * y
            r.xs[1, k, :, own_half] = following.astype(BF16)
            x_h0(1, k).start()
        else:
            rest = r.second[past] * r.y0[k] + r.second[past + 1] * y
            from_home(rest, r.blend1, r.cs_wide, k)
            c_mix(k).start()

    def mix():
        for k in chunks:
            c_mix(k).wait()
            r.blend1[theirs(k), :] = r.cv_wide[k]
        r.mixed_t[...] = (r.blend2_t[...] + r.blend1[...].T).astype(BF16)

    def grad_share(l, k):
        x_gy(k).wait()
        c_gy(k).start()

    def grad_whole(l, k):
        c_gy(k).wait()

    def feed_back(l, k):
        here = of(k)
        grad = nt(r.gy[here], r.wd[l])
        grad = (grad * r.slope[l, here].astype(F32)).astype(BF16)
        r.gp[here] = grad
        split_sum(k, nt(grad, r.wu[l]), c_bp(k))

    def back_sum(l, k):
        chip_sum(k, c_bp(k), r.crecv_bwd, x_arb(k))

    def mid_back(l, k):
        x_arb(k).wait()
        grad = r.acc[k] + r.xrecv_whole[k].astype(F32)
        z = r.z2[l, k].astype(F32)
        once = jnp.where(xx == 0, 1.0, 0.0)
        r.gains[2 + l : 3 + l, :] += once * fold(grad * z)
        grad = grad * r.gain_mlp[l : l + 1, :]
        total = r.gy[mine(k)].astype(F32) + center_back(grad, z, r.s2[l, k])
        r.mid[k] = of_chip(total)
        r.gm[mine(k)] = total.astype(BF16)
        c_gm(k).start()

    def heads_grad(l, k):
        c_gm(k).wait()
        r.grad_att[of(k)] = nt(r.gm[of(k)], r.wo[l]).astype(BF16)

    def attend_back(l, k, h):
        seen = (k + 1) * chunk
        here = of(k)
        lanes = slice(h * HEAD, (h + 1) * HEAD)
        grad = r.grad_att[here, lanes]
        inner_sum = jnp.sum(
            grad.astype(F32) * r.att[l, here, lanes].astype(F32), -1, keepdims=True
        )
        q, keys, vals = r.q[l, h, here, :], r.k[l, h, :seen, :], r.v[l, h, :seen, :]
        scores = nt(q, keys) + r.bias[here, :seen].astype(F32)
        probs = jnp.exp(scores - r.lse[l, here, h : h + 1])
        grad_scores = (probs * (nt(grad, vals) - inner_sum)).astype(BF16)
        grad_keys = tn(grad_scores, q)
        grad_vals = tn(probs.astype(BF16), grad)
        if k == count - 1:
            r.dqk[h, :, HEAD:] = grad_keys
            r.dv[:, lanes] = grad_vals
        else:
            r.dqk[h, :seen, HEAD:] += grad_keys
            r.dv[:seen, lanes] += grad_vals
        r.dqk[h, here, :HEAD] = nn(grad_scores, keys) * HEAD**-0.5

    def project_back(l, k):
        here = of(k)
        for h in range(heads):
            base = h * 3 * HEAD
            pair = turn(r.dqk[h, here, :], here, -1.0)
            r.dqkv[here, base : base + 2 * HEAD] = pair.astype(BF16)
            lanes = slice(h * HEAD, (h + 1) * HEAD)
            r.dqkv[here, base + 2 * HEAD : base + 3 * HEAD] = r.dv[here, lanes].astype(BF16)
        split_sum(k, nn(r.dqkv[here], r.wq[l]), c_np(k))

    def in_back(l, k):
        c_np(k).wait()
        grad = r.acc[k] + r.crecv_bwd[k].astype(F32)
        z = r.z1[l, k].astype(F32)
        r.gains[l : l + 1, :] += fold(grad * z)
        r.acc[k] = center_back(grad * r.gain_attn[l : l + 1, :], z, r.s1[l, k])
        r.xstage_half[k] = r.acc[k, :, far_half].astype(BF16)
        x_rsb(k).start()

    def block_back(l, k):
        x_rsb(k).wait()
        grad = r.mid[k] + r.acc[k, :, own_half] + r.xrecv_half[k].astype(F32)
        if l == 1:
            before = r.first[past] * grad + r.second[past] * r.cot_home[k].astype(F32)
            r.gy[mine(k), own_half] = before.astype(BF16)
            x_gy(k).start()
            from_home(grad, r.grad_next, r.cs_wide, k)
            c_gn(k).start()
            r.dots[past : past + 1, :half] += fold(r.y0[k] * grad)
        else:
            from_home(grad, r.grad_next, r.cs_gc, k)
            c_gc(k).start()

    def next_back():
        for k in chunks:
            c_gn(k).wait()
            r.grad_next[theirs(k), :] = r.cv_wide[k]
        r.grad_next_t[...] = r.grad_next[...].T

    def products(step):
        here = slice(step * strip, (step + 1) * strip)
        grad_next = r.grad_next_t[here, :]
        for j in range(past):
            r.dots[j : j + 1, :] += fold(r.hist[j, here, :].astype(F32) * grad_next)

    def current_back():
        for k in chunks:
            c_gc(k).wait()
            r.grad_next[theirs(k), :] = r.cv_gc[k].astype(F32)
        r.grad_current_t[...] = r.grad_next[...].T.astype(BF16)

    def keep_grad(piece, columns, values):
        for j in range(8):
            r.grads[piece, j % 2, j // 2, :, columns] = values[j * block : (j + 1) * block].astype(BF16)

    def grads_down(l):
        first = 6 * (1 - l)
        values = tn(r.gy[...], r.hid[l])
        keep_grad(first, slice(None), values[:, :half])
        y_start(first)
        keep_grad(first + 1, slice(None), values[:, half:])
        y_start(first + 1)

    def grads_up(l):
        first = 6 * (1 - l) + 2
        values = tn(r.n2[l], r.gp[...])
        keep_grad(first, slice(None), values[:, :half])
        y_start(first)
        keep_grad(first + 1, slice(None), values[:, half:])
        y_start(first + 1)

    def grads_attend(l):
        first = 6 * (1 - l) + 4
        values = tn(r.n1[l], r.dqkv[...])
        keep_grad(first, slice(None), values[:, :half])
        y_start(first)
        keep_grad(first + 1, slice(0, own_width), values[:, half:])
        keep_grad(first + 1, slice(own_width, half), tn(r.gm[...], r.att[l]))
        y_start(first + 1)

    def y_start(piece):
        if inner:
            y_copy(piece).start()

    def z_start(piece):
        if not inner:
            return
        y_copy(piece).wait()
        for z in range(4):
            both = r.grads[piece, yy, z].astype(F32) + r.y_in[piece, z].astype(F32)
            r.grads[piece, yy, z] = both.astype(BF16)
        for step in (2, 1, 3):
            z_copy(piece, step).start()

    def z_finish(piece):
        if not inner:
            return
        total = r.grads[piece, yy, zz].astype(F32)
        for step in (1, 2, 3):
            z_copy(piece, step).wait()
            total = total + r.z_in[piece, step - 1].astype(F32)
        r.parts[piece] = total

    def small_0():
        for i in range(width // 128):
            r.small[0, 4 * i : 4 * i + 4, :] = r.gains[:4, i * 128 : (i + 1) * 128]
        base = width // 32
        r.small[0, base : base + 32, :] = jnp.broadcast_to(
            jnp.sum(r.dots[...], -1, keepdims=True), (32, 128)
        )
        if inner:
            sm_copy(0, 0, core_peer).start()
        else:
            r.sums[...] = r.small[0]

    def small_next(stage, peer, onward):
        if not inner:
            return
        sm_copy(stage, stage, peer).wait()
        r.small[stage + 1] = r.small[stage] + r.small_in[stage]
        for slot, target in onward:
            sm_copy(stage + 1, slot, target).start()

    def small_1():
        small_next(0, core_peer, [(1, x_peer)])

    def small_2():
        small_next(1, x_peer, [(2, y_peer)])

    def small_3():
        small_next(2, y_peer, [*enumerate(z_peers, 3)])

    def small_4():
        if not inner:
            return
        for slot, target in enumerate(z_peers, 3):
            sm_copy(3, slot, target).wait()
        by_z = []
        for z in range(4):
            value = r.small[3]
            for step in (1, 2, 3):
                value = jnp.where(lax.rem(z + step, 4) == zz, r.small_in[2 + step], value)
            by_z.append(value)
        r.sums[...] = (by_z[0] + by_z[1]) + (by_z[2] + by_z[3])

    order = [
        (cur,), (turn_tables,), (cot,), (cur_home, 0), (blends, 0), (cur_home, 1), (cur_home, 3), (cur_home, 2),
        (cot_home, 3), (cot_home, 1), (cot_home, 2), (cot_home, 0), (blends, 1), (blends, 2), (norm_in, 0, 0),
        (blends, 3), (norm_in, 0, 1), (blend_send,), (project, 0, 0), (attend, 0, 0, 0), (attend, 0, 0, 1),
        (attend, 0, 0, 2), (project_out, 0, 0), (norm_in, 0, 2), (blend_home, 3), (norm_in, 0, 3), (project, 0, 1),
        (attend, 0, 1, 0), (attend, 0, 1, 2), (project, 0, 3), (out_sum, 0, 0), (attend, 0, 1, 1),
        (project_out, 0, 1), (project, 0, 2), (attend, 0, 3, 2), (attend, 0, 2, 2), (out_sum, 0, 1),
        (grad_share, 1, 2), (attend, 0, 2, 1), (grad_share, 1, 1), (attend, 0, 2, 0), (project_out, 0, 2),
        (attend, 0, 3, 0), (grad_whole, 1, 2), (attend, 0, 3, 1), (project_out, 0, 3), (out_sum, 0, 2),
        (grad_whole, 1, 1), (blend_home, 0), (blend_home, 2), (blend_home, 1), (grad_share, 1, 0), (grad_share, 1, 3),
        (norm_mid, 0, 0), (out_sum, 0, 3), (grad_whole, 1, 0), (norm_mid, 0, 1), (grad_whole, 1, 3), (feed, 0, 0),
        (feed, 0, 1), (norm_mid, 0, 2), (chip_scatter, 0, 0), (chip_scatter, 0, 1), (feed, 0, 2), (norm_mid, 0, 3),
        (block_out, 0, 0), (chip_scatter, 0, 2), (feed, 0, 3), (block_out, 0, 1), (chip_scatter, 0, 3),
        (norm_in, 1, 0), (block_out, 0, 2), (project, 1, 0), (attend, 1, 0, 2), (norm_in, 1, 1), (attend, 1, 0, 1),
        (attend, 1, 0, 0), (project_out, 1, 0), (block_out, 0, 3), (project, 1, 1), (attend, 1, 1, 2),
        (out_sum, 1, 0), (attend, 1, 1, 0), (attend, 1, 1, 1), (project_out, 1, 1), (norm_in, 1, 2), (norm_in, 1, 3),
        (out_sum, 1, 1), (project, 1, 2), (attend, 1, 2, 0), (project, 1, 3), (attend, 1, 3, 2), (attend, 1, 3, 0),
        (attend, 1, 3, 1), (project_out, 1, 3), (norm_mid, 1, 0), (attend, 1, 2, 1), (attend, 1, 2, 2),
        (project_out, 1, 2), (out_sum, 1, 3), (norm_mid, 1, 1), (feed, 1, 0), (out_sum, 1, 2), (feed, 1, 1),
        (chip_scatter, 1, 0), (chip_scatter, 1, 1), (norm_mid, 1, 3), (feed, 1, 3), (norm_mid, 1, 2),
        (block_out, 1, 0), (chip_scatter, 1, 3), (feed_back, 1, 0), (feed, 1, 2), (block_out, 1, 1),
        (feed_back, 1, 1), (back_sum, 1, 0), (grads_down, 1), (back_sum, 1, 1), (block_out, 1, 3),
        (chip_scatter, 1, 2), (feed_back, 1, 3), (back_sum, 1, 3), (mid_back, 1, 0), (mid_back, 1, 1),
        (block_out, 1, 2), (feed_back, 1, 2), (grads_up, 1), (z_start, 0), (back_sum, 1, 2), (mix,), (mid_back, 1, 3),
        (heads_grad, 1, 3), (attend_back, 1, 3, 1), (attend_back, 1, 3, 2), (attend_back, 1, 3, 0),
        (project_back, 1, 3), (mid_back, 1, 2), (z_start, 1), (in_back, 1, 3), (heads_grad, 1, 2),
        (attend_back, 1, 2, 1), (attend_back, 1, 2, 0), (attend_back, 1, 2, 2), (project_back, 1, 2),
        (heads_grad, 1, 1), (attend_back, 1, 1, 1), (attend_back, 1, 1, 0), (attend_back, 1, 1, 2),
        (block_back, 1, 3), (project_back, 1, 1), (in_back, 1, 2), (heads_grad, 1, 0), (attend_back, 1, 0, 1),
        (z_start, 2), (attend_back, 1, 0, 0), (attend_back, 1, 0, 2), (project_back, 1, 0), (in_back, 1, 1),
        (grads_attend, 1), (in_back, 1, 0), (grad_share, 0, 3), (z_finish, 0), (block_back, 1, 2), (z_finish, 1),
        (grad_whole, 0, 3), (feed_back, 0, 3), (block_back, 1, 1), (z_start, 3), (block_back, 1, 0), (back_sum, 0, 3),
        (grad_share, 0, 2), (next_back,), (products, 2), (products, 1), (grad_share, 0, 1), (products, 0),
        (z_finish, 2), (products, 3), (grad_share, 0, 0), (grad_whole, 0, 2), (feed_back, 0, 2), (grad_whole, 0, 1),
        (feed_back, 0, 1), (grad_whole, 0, 0), (z_start, 4), (grads_down, 0), (mid_back, 0, 3), (feed_back, 0, 0),
        (back_sum, 0, 1), (grads_up, 0), (back_sum, 0, 2), (back_sum, 0, 0), (heads_grad, 0, 3),
        (attend_back, 0, 3, 0), (attend_back, 0, 3, 1), (attend_back, 0, 3, 2), (project_back, 0, 3), (z_start, 5),
        (z_finish, 3), (mid_back, 0, 1), (in_back, 0, 3), (mid_back, 0, 2), (z_finish, 4), (heads_grad, 0, 2),
        (attend_back, 0, 2, 1), (attend_back, 0, 2, 0), (z_start, 6), (attend_back, 0, 2, 2), (project_back, 0, 2),
        (mid_back, 0, 0), (block_back, 0, 3), (heads_grad, 0, 1), (attend_back, 0, 1, 0), (attend_back, 0, 1, 2),
        (attend_back, 0, 1, 1), (project_back, 0, 1), (z_finish, 5), (heads_grad, 0, 0), (attend_back, 0, 0, 2),
        (attend_back, 0, 0, 1), (attend_back, 0, 0, 0), (project_back, 0, 0), (grads_attend, 0), (z_start, 7),
        (in_back, 0, 1), (in_back, 0, 0), (in_back, 0, 2), (small_0,), (small_1,), (z_finish, 6), (block_back, 0, 1),
        (block_back, 0, 0), (z_start, 8), (block_back, 0, 2), (small_2,), (current_back,), (z_finish, 7),
        (z_start, 9), (z_finish, 8), (z_start, 10), (z_finish, 9), (z_start, 11), (small_3,), (z_finish, 10),
        (z_finish, 11), (small_4,),
    ]
    for task, *where in order:
        task(*where)

    if not inner:
        out = pltpu.make_async_copy(r.grads, r.raw, r.load_sem.at[0])
        out.start()
        out.wait()


def finish(names, past, *refs):
    r = types.SimpleNamespace(**dict(zip(names, refs)))
    grad, grad_next = r.cotangent[...].astype(F32), r.grad_next_t[...]
    for j in range(past):
        r.grad_history[j] = (r.first[j] * grad_next + r.second[j] * grad).astype(BF16)
    r.mixed[...] = r.mixed_t[...]
    r.grad_current[...] = r.grad_current_t[...]
    width = r.grad_gain_attn.shape[1]
    for i in range(width // 128):
        lanes = slice(i * 128, (i + 1) * 128)
        r.grad_gain_attn[:, lanes] = r.sums[4 * i : 4 * i + 2, :]
        r.grad_gain_mlp[:, lanes] = r.sums[4 * i + 2 : 4 * i + 4, :]
    base = width // 32
    dots = r.sums[base : base + 32, :]
    for j in range(past + 1):
        r.grad_first[j] = dots[j, 0]
    for j in range(past + 2):
        r.grad_second[j] = dots[16 + j, 0]
    half, own_width = width // 2, width // 4
    for l in (0, 1):
        first = 6 * (1 - l)
        for i in (0, 1):
            lanes = slice(i * half, (i + 1) * half)
            r.grad_down[l, :, lanes] = r.parts[first + i]
            r.grad_up[l, :, lanes] = r.parts[first + 2 + i]
        r.grad_qkv[l, :, :half] = r.parts[first + 4]
        r.grad_qkv[l, :, half:] = r.parts[first + 5, :, :own_width]
        r.grad_out[l] = r.parts[first + 5, :, own_width:].T


def tables(rows):
    freqs = 10000.0 ** (-2.0 * np.arange(HEAD // 2) / HEAD)
    angles = np.arange(rows)[:, None] * np.tile(freqs, 4)[None, :]
    return np.cos(angles).astype(np.float32), np.sin(angles).astype(np.float32)


def shards(
    n_dp,
    current,
    history,
    cotangent,
    seq_lengths,
    w_qkv,
    w_out,
    w_up,
    w_down,
    gain_attn,
    gain_mlp,
    dwa_first,
    dwa_second,
):
    rows, own_width = current.shape
    past = history.shape[0]
    layers, width, _ = w_qkv.shape
    heads = w_out.shape[1] // HEAD
    units = w_up.shape[2]
    count = CHUNKS
    sub, half, block = rows // (2 * count), width // 2, width // 8
    inner = n_dp == 8
    cos_table, sin_table = tables(rows)

    hbm = pl.BlockSpec(memory_space=pl.ANY)
    vmem = pl.BlockSpec(memory_space=pltpu.VMEM)
    smem = pl.BlockSpec(memory_space=pltpu.SMEM)
    inputs = dict(
        current=(current.T, hbm),
        history=(history.transpose(0, 2, 1), hbm),
        cotangent=(cotangent.T, hbm),
        seq=(seq_lengths, smem),
        w_qkv=(w_qkv.transpose(0, 2, 1), hbm),
        w_out=(w_out, hbm),
        w_up=(w_up, hbm),
        w_down=(w_down, hbm),
        gain_attn=(gain_attn, vmem),
        gain_mlp=(gain_mlp, vmem),
        first=(dwa_first, smem),
        second=(dwa_second, smem),
        cos_table=(jnp.asarray(cos_table), hbm),
        sin_table=(jnp.asarray(sin_table), hbm),
    )

    def shape(dims, kind):
        return jax.ShapeDtypeStruct(dims, kind)

    small_rows = width // 32 + 32
    outputs = dict(
        mixed_t=(shape((own_width, rows), BF16), vmem),
        grad_current_t=(shape((own_width, rows), BF16), vmem),
        grad_next_t=(shape((own_width, rows), F32), vmem),
        sums=(shape((small_rows, 128), F32), vmem),
    )
    if inner:
        outputs.update(
            parts=(shape((6 * layers, block, half), F32), vmem),
        )
    else:
        outputs.update(
            raw=(shape((6 * layers, 2, 4, block, half), BF16), hbm),
        )

    def whole(kind=BF16, *lead):
        return pltpu.VMEM((*lead, rows, width), kind)

    def quarter(kind, *lead):
        return pltpu.VMEM((*lead, sub, width), kind)

    def quarter_half(kind, *lead):
        return pltpu.VMEM((*lead, sub, half), kind)

    def quarter_own(kind, *lead):
        return pltpu.VMEM((*lead, sub, own_width), kind)

    dma = pltpu.SemaphoreType.DMA
    scratch = dict(
        cur=pltpu.VMEM((rows, own_width), BF16),
        cot=pltpu.VMEM((rows, own_width), BF16),
        rope_cos=pltpu.VMEM((rows, 128), F32),
        rope_sin=pltpu.VMEM((rows, 128), F32),
        bias=pltpu.VMEM((rows, rows), BF16),
        wq=pltpu.VMEM((layers, 3 * own_width, width), BF16),
        wo=pltpu.VMEM(w_out.shape, BF16),
        wu=pltpu.VMEM(w_up.shape, BF16),
        wd=pltpu.VMEM(w_down.shape, BF16),
        cur_t=pltpu.VMEM((own_width, rows), BF16),
        cot_t=pltpu.VMEM((own_width, rows), BF16),
        hist=pltpu.VMEM((past, own_width, rows), BF16),
        blend1=pltpu.VMEM((rows, own_width), F32),
        blend2_t=pltpu.VMEM((own_width, rows), F32),
        grad_next=pltpu.VMEM((rows, own_width), F32),
        blend1_home=quarter_half(F32, count),
        home=quarter_half(F32),
        cot_home=quarter_half(BF16, count),
        y0=quarter_half(F32, count),
        xs=quarter(BF16, layers, count),
        z1=quarter(BF16, layers, count),
        z2=quarter(BF16, layers, count),
        s1=pltpu.VMEM((layers, count, sub, 1), F32),
        s2=pltpu.VMEM((layers, count, sub, 1), F32),
        acc=quarter(F32, count),
        mid=quarter_half(F32, count),
        n1=whole(BF16, layers),
        n2=whole(BF16, layers),
        hid=pltpu.VMEM((layers, rows, units), BF16),
        slope=pltpu.VMEM((layers, rows, units), BF16),
        gp=pltpu.VMEM((rows, units), BF16),
        gy=whole(),
        gm=whole(),
        q=pltpu.VMEM((layers, heads, rows, HEAD), BF16),
        k=pltpu.VMEM((layers, heads, rows, HEAD), BF16),
        v=pltpu.VMEM((layers, heads, rows, HEAD), BF16),
        att=pltpu.VMEM((layers, rows, own_width), BF16),
        lse=pltpu.VMEM((layers, rows, heads), F32),
        dqk=pltpu.VMEM((heads, rows, 2 * HEAD), F32),
        dv=pltpu.VMEM((rows, own_width), F32),
        dqkv=pltpu.VMEM((rows, 3 * own_width), BF16),
        gains=pltpu.VMEM((8, width), F32),
        dots=pltpu.VMEM((32, rows), F32),
        small=pltpu.VMEM((4, small_rows, 128), F32),
        small_in=pltpu.VMEM((6, small_rows, 128), F32),
        cstage=quarter(BF16, count),
        crecv_fwd=quarter(BF16, count),
        crecv_bwd=quarter(BF16, count),
        xstage=quarter(BF16, count),
        xrecv_whole=quarter(BF16, count),
        xstage_half=quarter_half(BF16, count),
        xrecv_half=quarter_half(BF16, count),
        cv_cur=quarter_own(BF16, count),
        cv_wide=quarter_own(F32, count),
        cs_wide=quarter_own(F32, count),
        grad_att=pltpu.VMEM((rows, own_width), BF16),
        cv_cot=quarter_own(BF16, count),
        cs_gc=quarter_own(BF16, count),
        cv_gc=quarter_own(BF16, count),
        grads=pltpu.VMEM((6 * layers, 2, 4, block, half), BF16),
        load_sem=dma((8,)),
        hist_in=dma((4,)),
        core_send=dma((14, count)),
        core_recv=dma((14, count)),
        x_send=dma((6, count)),
        x_recv=dma((6, count)),
    )
    if inner:
        scratch.update(
            y_in=pltpu.VMEM((6 * layers, 4, block, half), BF16),
            z_in=pltpu.VMEM((6 * layers, 3, block, half), BF16),
            y_send=dma((6 * layers,)),
            y_recv=dma((6 * layers,)),
            z_send=dma((6 * layers, 3)),
            z_recv=dma((6 * layers, 3)),
            sm_send=dma((6,)),
            sm_recv=dma((6,)),
        )
    names = [*inputs, *outputs, *scratch]
    results = pl.pallas_call(
        functools.partial(kernel, names, (rows, width, heads, units, past, count, inner)),
        out_shape=[o[0] for o in outputs.values()],
        in_specs=[i[1] for i in inputs.values()],
        out_specs=[o[1] for o in outputs.values()],
        scratch_shapes=[*scratch.values()],
        compiler_params=pltpu.CompilerParams(
            collective_id=0, has_side_effects=True, vmem_limit_bytes=int(63.5 * 2**20)
        ),
    )(*[i[0] for i in inputs.values()])
    out = types.SimpleNamespace(**dict(zip(outputs, results)))
    if not inner:
        out.sums = lax.psum(out.sums, ("dp", "mp"))

        raw = out.raw.transpose(0, 2, 1, 3, 4).reshape(6 * layers, width, half).astype(F32)
        out.parts = lax.psum_scatter(raw, "dp", scatter_dimension=1, tiled=True)
    share = out.parts.shape[1]
    given = dict(
        cotangent=(cotangent.T, vmem),
        first=(dwa_first, smem),
        second=(dwa_second, smem),
        mixed_t=(out.mixed_t, vmem),
        grad_current_t=(out.grad_current_t, vmem),
        grad_next_t=(out.grad_next_t, vmem),
        sums=(out.sums, vmem),
        parts=(out.parts, vmem),
    )
    wanted = dict(
        mixed=(shape((own_width, rows), BF16), vmem),
        grad_current=(shape((own_width, rows), BF16), vmem),
        grad_history=(shape((past, own_width, rows), BF16), vmem),
        grad_qkv=(shape((layers, share, 3 * own_width), F32), vmem),
        grad_out=(shape((layers, own_width, share), F32), vmem),
        grad_up=(shape((layers, share, units), F32), vmem),
        grad_down=(shape((layers, share, units), F32), vmem),
        grad_gain_attn=(shape((layers, width), F32), vmem),
        grad_gain_mlp=(shape((layers, width), F32), vmem),
        grad_first=(shape((past + 1,), F32), smem),
        grad_second=(shape((past + 2,), F32), smem),
    )
    results = pl.pallas_call(
        functools.partial(finish, [*given, *wanted], past),
        out_shape=[o[0] for o in wanted.values()],
        in_specs=[i[1] for i in given.values()],
        out_specs=[o[1] for o in wanted.values()],
        compiler_params=pltpu.CompilerParams(vmem_limit_bytes=62 * 2**20),
    )(*[i[0] for i in given.values()])
    out = types.SimpleNamespace(**dict(zip(wanted, results)))
    return (
        out.mixed.T,
        out.grad_current.T,
        out.grad_history.transpose(0, 2, 1),
        out.grad_qkv,
        out.grad_out,
        out.grad_up,
        out.grad_down.transpose(0, 2, 1),
        out.grad_gain_attn,
        out.grad_gain_mlp,
        out.grad_first,
        out.grad_second,
    )


def solution(mesh):
    in_specs = (
        P("dp", "mp"),
        P(None, "dp", "mp"),
        P("dp", "mp"),
        P("dp", None),
        P(None, None, "mp"),
        P(None, "mp", None),
        P(None, None, "mp"),
        P(None, "mp", None),
        P(),
        P(),
        P(),
        P(),
    )
    out_specs = (
        P("dp", "mp"),
        P("dp", "mp"),
        P(None, "dp", "mp"),
        P(None, "dp", "mp"),
        P(None, "mp", "dp"),
        P(None, "dp", "mp"),
        P(None, "mp", "dp"),
        P(),
        P(),
        P(),
        P(),
    )
    return jax.shard_map(
        functools.partial(shards, mesh.shape["dp"]),
        mesh=mesh,
        in_specs=in_specs,
        out_specs=out_specs,
        check_vma=False,
    )
```

```python
import functools
import types

import jax
import jax.numpy as jnp
import numpy as np
from jax import lax
from jax.experimental import pallas as pl
from jax.experimental.pallas import tpu as pltpu
from jax.sharding import PartitionSpec as P

HEAD = 64
EPS = 1e-05
F32 = jnp.float32
BF16 = jnp.bfloat16
MESH = pl.DeviceIdType.MESH
CHUNKS = 4
GELU_A = 0.7978845608
GELU_B = 0.044715
HIDDEN_AXES = (((1,), (0,)), ((), ()))
SHARED_AXES = (((1,), (1,)), ((), ()))
TOKEN_AXES = (((0,), (0,)), ((), ()))

def nn(a, b):
    return lax.dot_general(a, b, HIDDEN_AXES, preferred_element_type=F32)


def nt(a, b):
    return lax.dot_general(a, b, SHARED_AXES, preferred_element_type=F32)


def tn(a, b):
    return lax.dot_general(a, b, TOKEN_AXES, preferred_element_type=F32)


def center(values):
    shifted = values - jnp.mean(values, -1, keepdims=True)
    scale = lax.rsqrt(jnp.mean(shifted * shifted, -1, keepdims=True) + EPS)
    return shifted * scale, scale


def center_back(e, z, scale):
    return (e - jnp.mean(e, -1, keepdims=True) - z * jnp.mean(e * z, -1, keepdims=True)) * scale


def loop(count, step):
    def one(i, carry):
        step(i)
        return carry

    lax.fori_loop(0, count, one, 0)


def kernel(names, cfg, *refs):
    r = types.SimpleNamespace(**dict(zip(names, refs)))
    rows, width, heads, units, past, count, inner = cfg
    half, own_width = width // 2, width // 4
    chunk, sub = rows // count, rows // (2 * count)
    block, strip = width // 8, own_width // 4
    chunks = range(count)

    m = lax.axis_index("mp")
    core, xx = lax.rem(m, 2), m // 2
    core_peer = {"mp": m + 1 - 2 * core}
    x_peer = {"mp": lax.rem(m + 2, 4)}
    y_peer, z_peers = None, []
    if inner:
        d = lax.axis_index("dp")
        yy, zz = lax.rem(d, 2), d // 2
        y_peer = {"dp": d + 1 - 2 * yy}
        z_peers = [{"dp": lax.rem(d + 2 * step, 8)} for step in (1, 2, 3)]
    own_half = pl.ds(pl.multiple_of(xx * half, 128), half)
    far_half = pl.ds(pl.multiple_of((1 - xx) * half, 128), half)

    def of(k):
        return slice(k * chunk, (k + 1) * chunk)

    def mine(k):
        return pl.ds(pl.multiple_of(k * chunk + core * sub, 16), sub)

    def theirs(k):
        return pl.ds(pl.multiple_of(k * chunk + (1 - core) * sub, 16), sub)

    loads = []
    for index, (src, dst) in enumerate(
        (
            (r.current, r.cur_t),
            (r.cotangent, r.cot_t),
            (r.cos_table, r.rope_cos),
            (r.sin_table, r.rope_sin),
            (r.w_qkv, r.wq),
            (r.w_out, r.wo),
            (r.w_up, r.wu),
            (r.w_down, r.wd),
        )
    ):
        loads.append(pltpu.make_async_copy(src, dst, r.load_sem.at[index]))
    for index in (0, 2, 3, 1):
        loads[index].start()
    history = []
    for step in range(4):
        here = slice(step * strip, (step + 1) * strip)
        history.append(
            pltpu.make_async_copy(
                r.history.at[:, here, :], r.hist.at[:, here, :], r.hist_in.at[step]
            )
        )
        history[step].start()
    for load in loads[4:]:
        load.start()

    barrier = pltpu.get_barrier_semaphore()
    peers = [core_peer, x_peer] + ([y_peer] + z_peers if inner else [])
    for peer in peers:
        pl.semaphore_signal(barrier, inc=1, device_id=peer, device_id_type=MESH)
    pl.semaphore_wait(barrier, len(peers))

    def remote(src, dst, send, recv, peer):
        return pltpu.make_async_remote_copy(
            src_ref=src,
            dst_ref=dst,
            send_sem=send,
            recv_sem=recv,
            device_id=peer,
            device_id_type=MESH,
        )

    def over_core(kind, k, src, dst):
        return remote(src, dst, r.core_send.at[kind, k], r.core_recv.at[kind, k], core_peer)

    def over_x(kind, k, src, dst):
        return remote(src, dst, r.x_send.at[kind, k], r.x_recv.at[kind, k], x_peer)

    def c_cur(k):
        return over_core(0, k, r.cur.at[theirs(k)], r.cv_cur.at[k])

    def c_cot(k):
        return over_core(1, k, r.cot.at[theirs(k)], r.cv_cot.at[k])

    def c_b1(k):
        return over_core(2, k, r.blend1.at[theirs(k)], r.cv_wide.at[k])

    def c_n1(l, k):
        return over_core(3, k, r.n1.at[l, mine(k)], r.n1.at[l, mine(k)])

    def c_out(k):
        return over_core(4, k, r.cstage.at[k], r.crecv_fwd.at[k])

    def c_n2(l, k):
        return over_core(5, k, r.n2.at[l, mine(k)], r.n2.at[l, mine(k)])

    def c_dn(k):
        return over_core(6, k, r.cstage.at[k], r.crecv_fwd.at[k])

    def c_mix(k):
        return over_core(7, k, r.cs_wide.at[k], r.cv_wide.at[k])

    def c_gy(k):
        return over_core(8, k, r.gy.at[mine(k)], r.gy.at[mine(k)])

    def c_bp(k):
        return over_core(9, k, r.cstage.at[k], r.crecv_bwd.at[k])

    def c_gm(k):
        return over_core(10, k, r.gm.at[mine(k)], r.gm.at[mine(k)])

    def c_np(k):
        return over_core(11, k, r.cstage.at[k], r.crecv_bwd.at[k])

    def c_gn(k):
        return over_core(12, k, r.cs_wide.at[k], r.cv_wide.at[k])

    def c_gc(k):
        return over_core(13, k, r.cs_gc.at[k], r.cv_gc.at[k])

    def x_h0(l, k):
        return over_x(0, k, r.xs.at[l, k, :, own_half], r.xs.at[l, k, :, own_half])

    def x_ar(k):
        return over_x(1, k, r.xstage.at[k], r.xrecv_whole.at[k])

    def x_rs(k):
        return over_x(2, k, r.xstage_half.at[k], r.xrecv_half.at[k])

    def x_gy(k):
        return over_x(3, k, r.gy.at[mine(k), own_half], r.gy.at[mine(k), own_half])

    def x_arb(k):
        return over_x(4, k, r.xstage.at[k], r.xrecv_whole.at[k])

    def x_rsb(k):
        return over_x(5, k, r.xstage_half.at[k], r.xrecv_half.at[k])

    def y_copy(piece):
        return remote(
            r.grads.at[piece, 1 - yy],
            r.y_in.at[piece],
            r.y_send.at[piece],
            r.y_recv.at[piece],
            y_peer,
        )

    def z_copy(piece, step):
        return remote(
            r.grads.at[piece, yy, lax.rem(zz + step, 4)],
            r.z_in.at[piece, step - 1],
            r.z_send.at[piece, step - 1],
            r.z_recv.at[piece, step - 1],
            z_peers[step - 1],
        )

    def sm_copy(stage, slot, peer):
        return remote(
            r.small.at[stage], r.small_in.at[slot], r.sm_send.at[slot], r.sm_recv.at[slot], peer
        )

    def to_home(feature, recv, k):
        own, other = feature[mine(k), :].astype(F32), recv[k].astype(F32)
        first = core == 0
        r.home[:, :own_width] = jnp.where(first, own, other)
        r.home[:, own_width:] = jnp.where(first, other, own)
        return r.home[...]

    def from_home(values, keep, stage, k):
        first = core == 0
        low, high = values[:, :own_width], values[:, own_width:]
        keep[mine(k), :] = jnp.where(first, low, high).astype(keep.dtype)
        stage[k] = jnp.where(first, high, low).astype(stage.dtype)

    def of_chip(values):
        return jnp.where(xx == 0, values[:, :half], values[:, half:])

    def fold(values):
        return jnp.sum(values, 0, keepdims=True)

    def cur():
        loads[0].wait()
        r.cur[...] = r.cur_t[...].astype(F32).T.astype(BF16)
        for k in chunks:
            c_cur(k).start()

    def cot():
        loads[1].wait()
        r.cot[...] = r.cot_t[...].astype(F32).T.astype(BF16)
        for k in reversed(chunks):
            c_cot(k).start()
        r.gains[...] = jnp.zeros_like(r.gains)
        r.dots[...] = jnp.zeros_like(r.dots)

    def cur_home(k):
        c_cur(k).wait()
        r.xs[0, k, :, own_half] = to_home(r.cur, r.cv_cur, k).astype(BF16)
        x_h0(0, k).start()

    def cot_home(k):
        c_cot(k).wait()
        home = to_home(r.cot, r.cv_cot, k)
        r.cot_home[k] = home.astype(BF16)
        r.gy[mine(k), own_half] = (r.second[past + 1] * home).astype(BF16)
        x_gy(k).start()

    def turn_tables():
        loads[2].wait()
        loads[3].wait()
        segs = r.seq.shape[1]
        starts, ends = [], []
        total = jnp.int32(0)
        for index in range(segs):
            starts.append(total)
            total = total + r.seq[0, index]
            ends.append(total)
        cos_start = [r.rope_cos[pl.ds(jnp.clip(s, 0, rows - 1), 1), :] for s in starts]
        sin_start = [r.rope_sin[pl.ds(jnp.clip(s, 0, rows - 1), 1), :] for s in starts]
        size = rows // 4

        def part(i):
            here = pl.ds(pl.multiple_of(i * size, 16), size)
            place = lax.broadcasted_iota(jnp.int32, (size, 128), 0) + i * size
            lane = lax.broadcasted_iota(jnp.int32, (size, 128), 1)
            line = lax.broadcasted_iota(jnp.int32, (size, 1), 0) + i * size
            cos_s = jnp.broadcast_to(cos_start[0], (size, 128))
            sin_s = jnp.broadcast_to(sin_start[0], (size, 128))
            begin = jnp.zeros((size, 1), jnp.int32)
            for index in range(1, segs):
                inside = place >= ends[index - 1]
                cos_s = jnp.where(inside, cos_start[index], cos_s)
                sin_s = jnp.where(inside, sin_start[index], sin_s)
                begin = jnp.where(line >= ends[index - 1], starts[index], begin)
            cos_t, sin_t = r.rope_cos[here, :], r.rope_sin[here, :]
            sine = sin_t * cos_s - cos_t * sin_s
            r.rope_cos[here, :] = cos_t * cos_s + sin_t * sin_s
            r.rope_sin[here, :] = jnp.where(lax.rem(lane, HEAD) < HEAD // 2, -sine, sine)
            query = lax.broadcasted_iota(jnp.int32, (size, rows), 0) + i * size
            key = lax.broadcasted_iota(jnp.int32, (size, rows), 1)
            r.bias[here, :] = jnp.where((key <= query) & (key >= begin), 0.0, -1e30).astype(BF16)

        loop(4, part)

    def turn(values, here, sign):
        lane = lax.broadcasted_iota(jnp.int32, values.shape, 1)
        other = jnp.where(
            lax.rem(lane, HEAD) < HEAD // 2,
            pltpu.roll(values, 128 - HEAD // 2, 1),
            pltpu.roll(values, HEAD // 2, 1),
        )
        return values * r.rope_cos[here, :] + sign * (other * r.rope_sin[here, :])

    def blends(step):
        here = slice(step * strip, (step + 1) * strip)
        history[step].wait()
        grad = r.cot_t[here, :].astype(F32)

        def add(j, sums):
            one, two = sums
            value = r.hist[j, here, :].astype(F32)
            line = pl.ds(16 + j, 1)
            r.dots[line, :] += fold(value * grad)
            return one + r.first[j] * value, two + r.second[j] * value

        zeros = jnp.zeros((strip, rows), F32)
        one, two = lax.fori_loop(0, past, add, (zeros, zeros))
        r.grad_next_t[here, :] = one
        r.blend2_t[here, :] = two

    def blend_send():
        r.blend1[...] = r.grad_next_t[...].T
        for k in chunks:
            c_b1(k).start()

    def blend_home(k):
        c_b1(k).wait()
        r.blend1_home[k] = to_home(r.blend1, r.cv_wide, k)

    def norm_in(l, k):
        x_h0(l, k).wait()
        z, scale = center(r.xs[l, k].astype(F32))
        r.z1[l, k] = z.astype(BF16)
        r.s1[l, k] = scale
        r.n1[l, mine(k)] = (z * r.gain_attn[l : l + 1, :]).astype(BF16)
        c_n1(l, k).start()

    def project(l, k):
        if (l, k) == (0, 0):
            for load in loads[4:]:
                load.wait()
        c_n1(l, k).wait()
        here = of(k)
        acc = nt(r.n1[l, here], r.wq[l])
        for h in range(heads):
            base = h * 3 * HEAD
            pair = turn(acc[:, base : base + 2 * HEAD], here, 1.0)
            r.q[l, h, here, :] = (pair[:, :HEAD] * HEAD**-0.5).astype(BF16)
            r.k[l, h, here, :] = pair[:, HEAD:].astype(BF16)
            r.v[l, h, here, :] = acc[:, base + 2 * HEAD : base + 3 * HEAD].astype(BF16)

    def attend(l, k, h):
        seen = (k + 1) * chunk
        here = of(k)
        scores = nt(r.q[l, h, here, :], r.k[l, h, :seen, :]) + r.bias[here, :seen].astype(F32)
        top = jnp.max(scores, -1, keepdims=True)
        probs = jnp.exp(scores - top)
        total = jnp.sum(probs, -1, keepdims=True)
        result = nn(probs.astype(BF16), r.v[l, h, :seen, :]) / total
        r.att[l, here, h * HEAD : (h + 1) * HEAD] = result.astype(BF16)
        r.lse[l, here, h : h + 1] = top + jnp.log(total)

    def split_sum(k, total, send):
        for who in (0, 1):

            @pl.when(core == who)
            def _(who=who):
                other = slice((1 - who) * sub, (2 - who) * sub)
                own = slice(who * sub, (who + 1) * sub)
                r.cstage[k] = total[other].astype(BF16)
                send.start()
                r.acc[k] = total[own]

    def chip_sum(k, arrival, received, onward):
        arrival.wait()
        total = r.acc[k] + received[k].astype(F32)
        r.acc[k] = total
        r.xstage[k] = total.astype(BF16)
        onward.start()

    def project_out(l, k):
        split_sum(k, nn(r.att[l, of(k)], r.wo[l]), c_out(k))

    def out_sum(l, k):
        chip_sum(k, c_out(k), r.crecv_fwd, x_ar(k))

    def norm_mid(l, k):
        x_ar(k).wait()
        middle = r.xs[l, k].astype(F32) + r.acc[k] + r.xrecv_whole[k].astype(F32)
        r.mid[k] = of_chip(middle)
        z, scale = center(middle)
        r.z2[l, k] = z.astype(BF16)
        r.s2[l, k] = scale
        r.n2[l, mine(k)] = (z * r.gain_mlp[l : l + 1, :]).astype(BF16)
        c_n2(l, k).start()

    def feed(l, k):
        c_n2(l, k).wait()
        here = of(k)
        pre = nn(r.n2[l, here], r.wu[l])
        square = pre * pre
        wave = jnp.tanh(pre * (GELU_A + GELU_A * GELU_B * square))
        left = 0.5 + 0.5 * wave
        hidden = (pre * left).astype(BF16)
        slope = left + (0.5 - 0.5 * wave * wave) * pre * (
            GELU_A + 3.0 * GELU_A * GELU_B * square
        )
        r.hid[l, here] = hidden
        r.slope[l, here] = slope.astype(BF16)
        split_sum(k, nn(hidden, r.wd[l]), c_dn(k))

    def chip_scatter(l, k):
        c_dn(k).wait()
        far = r.acc[k, :, far_half] + r.crecv_fwd[k, :, far_half].astype(F32)
        r.xstage_half[k] = far.astype(BF16)
        x_rs(k).start()

    def block_out(l, k):
        x_rs(k).wait()
        y = (
            r.mid[k]
            + r.acc[k, :, own_half]
            + r.crecv_fwd[k, :, own_half].astype(F32)
            + r.xrecv_half[k].astype(F32)
        )
        line = 16 + past + l
        r.dots[line : line + 1, :half] += fold(y * r.cot_home[k].astype(F32))
        if l == 0:
            r.y0[k] = y
            following = r.blend1_home[k] + r.first[past] * y
            r.xs[1, k, :, own_half] = following.astype(BF16)
            x_h0(1, k).start()
        else:
            rest = r.second[past] * r.y0[k] + r.second[past + 1] * y
            from_home(rest, r.blend1, r.cs_wide, k)
            c_mix(k).start()

    def mix():
        for k in chunks:
            c_mix(k).wait()
            r.blend1[theirs(k), :] = r.cv_wide[k]
        r.mixed_t[...] = (r.blend2_t[...] + r.blend1[...].T).astype(BF16)

    def grad_share(l, k):
        x_gy(k).wait()
        c_gy(k).start()

    def grad_whole(l, k):
        c_gy(k).wait()

    def feed_back(l, k):
        here = of(k)
        grad = nt(r.gy[here], r.wd[l])
        grad = (grad * r.slope[l, here].astype(F32)).astype(BF16)
        r.gp[here] = grad
        split_sum(k, nt(grad, r.wu[l]), c_bp(k))

    def back_sum(l, k):
        chip_sum(k, c_bp(k), r.crecv_bwd, x_arb(k))

    def mid_back(l, k):
        x_arb(k).wait()
        grad = r.acc[k] + r.xrecv_whole[k].astype(F32)
        z = r.z2[l, k].astype(F32)
        once = jnp.where(xx == 0, 1.0, 0.0)
        r.gains[2 + l : 3 + l, :] += once * fold(grad * z)
        grad = grad * r.gain_mlp[l : l + 1, :]
        total = r.gy[mine(k)].astype(F32) + center_back(grad, z, r.s2[l, k])
        r.mid[k] = of_chip(total)
        r.gm[mine(k)] = total.astype(BF16)
        c_gm(k).start()

    def heads_grad(l, k):
        c_gm(k).wait()
        r.grad_att[of(k)] = nt(r.gm[of(k)], r.wo[l]).astype(BF16)

    def attend_back(l, k, h):
        seen = (k + 1) * chunk
        here = of(k)
        lanes = slice(h * HEAD, (h + 1) * HEAD)
        grad = r.grad_att[here, lanes]
        inner_sum = jnp.sum(
            grad.astype(F32) * r.att[l, here, lanes].astype(F32), -1, keepdims=True
        )
        q, keys, vals = r.q[l, h, here, :], r.k[l, h, :seen, :], r.v[l, h, :seen, :]
        scores = nt(q, keys) + r.bias[here, :seen].astype(F32)
        probs = jnp.exp(scores - r.lse[l, here, h : h + 1])
        grad_scores = (probs * (nt(grad, vals) - inner_sum)).astype(BF16)
        grad_keys = tn(grad_scores, q)
        grad_vals = tn(probs.astype(BF16), grad)
        if k == count - 1:
            r.dqk[h, :, HEAD:] = grad_keys
            r.dv[:, lanes] = grad_vals
        else:
            r.dqk[h, :seen, HEAD:] += grad_keys
            r.dv[:seen, lanes] += grad_vals
        r.dqk[h, here, :HEAD] = nn(grad_scores, keys) * HEAD**-0.5

    def project_back(l, k):
        here = of(k)
        for h in range(heads):
            base = h * 3 * HEAD
            pair = turn(r.dqk[h, here, :], here, -1.0)
            r.dqkv[here, base : base + 2 * HEAD] = pair.astype(BF16)
            lanes = slice(h * HEAD, (h + 1) * HEAD)
            r.dqkv[here, base + 2 * HEAD : base + 3 * HEAD] = r.dv[here, lanes].astype(BF16)
        split_sum(k, nn(r.dqkv[here], r.wq[l]), c_np(k))

    def in_back(l, k):
        c_np(k).wait()
        grad = r.acc[k] + r.crecv_bwd[k].astype(F32)
        z = r.z1[l, k].astype(F32)
        r.gains[l : l + 1, :] += fold(grad * z)
        r.acc[k] = center_back(grad * r.gain_attn[l : l + 1, :], z, r.s1[l, k])
        r.xstage_half[k] = r.acc[k, :, far_half].astype(BF16)
        x_rsb(k).start()

    def block_back(l, k):
        x_rsb(k).wait()
        grad = r.mid[k] + r.acc[k, :, own_half] + r.xrecv_half[k].astype(F32)
        if l == 1:
            before = r.first[past] * grad + r.second[past] * r.cot_home[k].astype(F32)
            r.gy[mine(k), own_half] = before.astype(BF16)
            x_gy(k).start()
            from_home(grad, r.grad_next, r.cs_wide, k)
            c_gn(k).start()
            r.dots[past : past + 1, :half] += fold(r.y0[k] * grad)
        else:
            from_home(grad, r.grad_next, r.cs_gc, k)
            c_gc(k).start()

    def next_back():
        for k in chunks:
            c_gn(k).wait()
            r.grad_next[theirs(k), :] = r.cv_wide[k]
        r.grad_next_t[...] = r.grad_next[...].T

    def products(step):
        here = slice(step * strip, (step + 1) * strip)
        grad_next = r.grad_next_t[here, :]

        def add(j):
            line = pl.ds(j, 1)
            r.dots[line, :] += fold(r.hist[j, here, :].astype(F32) * grad_next)

        loop(past, add)

    def current_back():
        for k in chunks:
            c_gc(k).wait()
            r.grad_next[theirs(k), :] = r.cv_gc[k].astype(F32)
        r.grad_current_t[...] = r.grad_next[...].T.astype(BF16)

    def keep_grad(piece, columns, values):
        for j in range(8):
            r.grads[piece, j % 2, j // 2, :, columns] = values[j * block : (j + 1) * block].astype(BF16)

    def grads_down(l):
        first = 6 * (1 - l)

        def part(i):
            lanes = pl.ds(pl.multiple_of(i * half, 128), half)
            keep_grad(first + i, slice(None), tn(r.gy[...], r.hid[l, :, lanes]))
            y_start(first + i)

        loop(2, part)

    def grads_up(l):
        first = 6 * (1 - l) + 2

        def part(i):
            lanes = pl.ds(pl.multiple_of(i * half, 128), half)
            keep_grad(first + i, slice(None), tn(r.n2[l], r.gp[:, lanes]))
            y_start(first + i)

        loop(2, part)

    def grads_attend(l):
        first = 6 * (1 - l) + 4
        values = tn(r.n1[l], r.dqkv[...])
        keep_grad(first, slice(None), values[:, :half])
        y_start(first)
        keep_grad(first + 1, slice(0, own_width), values[:, half:])
        keep_grad(first + 1, slice(own_width, half), tn(r.gm[...], r.att[l]))
        y_start(first + 1)

    def y_start(piece):
        if inner:
            y_copy(piece).start()

    def z_start(piece):
        if not inner:
            return
        y_copy(piece).wait()

        def add(z):
            both = r.grads[piece, yy, z].astype(F32) + r.y_in[piece, z].astype(F32)
            r.grads[piece, yy, z] = both.astype(BF16)

        loop(4, add)
        for step in (2, 1, 3):
            z_copy(piece, step).start()

    def z_finish(piece):
        if not inner:
            return
        for step in (1, 2, 3):
            z_copy(piece, step).wait()

        def add(i):
            here = pl.ds(pl.multiple_of(i * 32, 32), 32)
            total = r.grads[piece, yy, zz, here].astype(F32)
            for step in range(3):
                total = total + r.z_in[piece, step, here].astype(F32)
            r.parts[piece, here] = total

        loop(block // 32, add)

    def small_0():
        for i in range(width // 128):
            r.small[0, 4 * i : 4 * i + 4, :] = r.gains[:4, i * 128 : (i + 1) * 128]
        base = width // 32
        r.small[0, base : base + 32, :] = jnp.broadcast_to(
            jnp.sum(r.dots[...], -1, keepdims=True), (32, 128)
        )
        if inner:
            sm_copy(0, 0, core_peer).start()
        else:
            r.sums[...] = r.small[0]

    def small_next(stage, peer, onward):
        if not inner:
            return
        sm_copy(stage, stage, peer).wait()
        r.small[stage + 1] = r.small[stage] + r.small_in[stage]
        for slot, target in onward:
            sm_copy(stage + 1, slot, target).start()

    def small_1():
        small_next(0, core_peer, [(1, x_peer)])

    def small_2():
        small_next(1, x_peer, [(2, y_peer)])

    def small_3():
        small_next(2, y_peer, [*enumerate(z_peers, 3)])

    def small_4():
        if not inner:
            return
        for slot, target in enumerate(z_peers, 3):
            sm_copy(3, slot, target).wait()
        by_z = []
        for z in range(4):
            value = r.small[3]
            for step in (1, 2, 3):
                value = jnp.where(lax.rem(z + step, 4) == zz, r.small_in[2 + step], value)
            by_z.append(value)
        r.sums[...] = (by_z[0] + by_z[1]) + (by_z[2] + by_z[3])

    order = [
        (cur,), (turn_tables,), (cot,), (blends, 0), (cur_home, 0), (cur_home, 1), (cur_home, 3), (cur_home, 2),
        (blends, 1), (cot_home, 3), (cot_home, 2), (cot_home, 0), (blends, 2), (blends, 3), (blend_send,),
        (cot_home, 1), (norm_in, 0, 0), (blend_home, 0), (blend_home, 1), (blend_home, 2), (norm_in, 0, 1),
        (blend_home, 3), (project, 0, 0), (attend, 0, 0, 0), (attend, 0, 0, 1), (attend, 0, 0, 2), (project, 0, 1),
        (project_out, 0, 0), (attend, 0, 1, 1), (norm_in, 0, 2), (attend, 0, 1, 0), (norm_in, 0, 3),
        (grad_share, 1, 3), (attend, 0, 1, 2), (project_out, 0, 1), (out_sum, 0, 0), (project, 0, 2),
        (attend, 0, 2, 0), (attend, 0, 2, 1), (out_sum, 0, 1), (grad_whole, 1, 3), (grad_share, 1, 2),
        (attend, 0, 2, 2), (project_out, 0, 2), (grad_share, 1, 0), (project, 0, 3), (attend, 0, 3, 1),
        (attend, 0, 3, 0), (grad_share, 1, 1), (attend, 0, 3, 2), (project_out, 0, 3), (grad_whole, 1, 2),
        (out_sum, 0, 2), (grad_whole, 1, 0), (norm_mid, 0, 0), (grad_whole, 1, 1), (out_sum, 0, 3), (feed, 0, 0),
        (norm_mid, 0, 1), (chip_scatter, 0, 0), (feed, 0, 1), (norm_mid, 0, 2), (chip_scatter, 0, 1), (feed, 0, 2),
        (norm_mid, 0, 3), (block_out, 0, 0), (chip_scatter, 0, 2), (feed, 0, 3), (block_out, 0, 1),
        (chip_scatter, 0, 3), (norm_in, 1, 0), (block_out, 0, 2), (project, 1, 0), (attend, 1, 0, 0), (norm_in, 1, 1),
        (attend, 1, 0, 1), (attend, 1, 0, 2), (project_out, 1, 0), (block_out, 0, 3), (project, 1, 1),
        (attend, 1, 1, 0), (attend, 1, 1, 2), (attend, 1, 1, 1), (project_out, 1, 1), (norm_in, 1, 2),
        (out_sum, 1, 0), (out_sum, 1, 1), (norm_in, 1, 3), (project, 1, 2), (attend, 1, 2, 2), (attend, 1, 2, 0),
        (attend, 1, 2, 1), (project, 1, 3), (attend, 1, 3, 2), (attend, 1, 3, 1), (attend, 1, 3, 0),
        (project_out, 1, 3), (norm_mid, 1, 0), (project_out, 1, 2), (out_sum, 1, 3), (feed, 1, 0), (norm_mid, 1, 1),
        (out_sum, 1, 2), (chip_scatter, 1, 0), (feed, 1, 1), (norm_mid, 1, 3), (chip_scatter, 1, 1), (feed, 1, 3),
        (norm_mid, 1, 2), (block_out, 1, 0), (feed_back, 1, 0), (chip_scatter, 1, 3), (feed, 1, 2), (block_out, 1, 1),
        (feed_back, 1, 1), (back_sum, 1, 0), (grads_down, 1), (chip_scatter, 1, 2), (back_sum, 1, 1),
        (block_out, 1, 3), (feed_back, 1, 3), (back_sum, 1, 3), (mid_back, 1, 0), (block_out, 1, 2),
        (feed_back, 1, 2), (grads_up, 1), (mix,), (back_sum, 1, 2), (mid_back, 1, 1), (z_start, 0), (mid_back, 1, 3),
        (heads_grad, 1, 3), (attend_back, 1, 3, 0), (attend_back, 1, 3, 1), (mid_back, 1, 2), (attend_back, 1, 3, 2),
        (project_back, 1, 3), (z_start, 1), (heads_grad, 1, 2), (attend_back, 1, 2, 0), (attend_back, 1, 2, 2),
        (attend_back, 1, 2, 1), (in_back, 1, 3), (project_back, 1, 2), (heads_grad, 1, 1), (attend_back, 1, 1, 1),
        (attend_back, 1, 1, 2), (attend_back, 1, 1, 0), (project_back, 1, 1), (in_back, 1, 2), (heads_grad, 1, 0),
        (attend_back, 1, 0, 1), (attend_back, 1, 0, 2), (attend_back, 1, 0, 0), (project_back, 1, 0), (z_start, 2),
        (block_back, 1, 3), (grads_attend, 1), (z_finish, 0), (in_back, 1, 1), (in_back, 1, 0), (block_back, 1, 2),
        (z_finish, 1), (grad_share, 0, 3), (block_back, 1, 1), (z_start, 3), (grad_whole, 0, 3), (feed_back, 0, 3),
        (block_back, 1, 0), (grad_share, 0, 2), (back_sum, 0, 3), (next_back,), (products, 0), (products, 3),
        (products, 1), (grad_whole, 0, 2), (grad_share, 0, 1), (z_finish, 2), (feed_back, 0, 2), (products, 2),
        (grad_share, 0, 0), (z_start, 4), (grad_whole, 0, 1), (feed_back, 0, 1), (back_sum, 0, 2), (grad_whole, 0, 0),
        (feed_back, 0, 0), (mid_back, 0, 3), (grads_down, 0), (back_sum, 0, 1), (grads_up, 0), (back_sum, 0, 0),
        (heads_grad, 0, 3), (attend_back, 0, 3, 2), (attend_back, 0, 3, 1), (z_start, 5), (mid_back, 0, 2),
        (attend_back, 0, 3, 0), (project_back, 0, 3), (z_finish, 3), (heads_grad, 0, 2), (attend_back, 0, 2, 0),
        (attend_back, 0, 2, 2), (mid_back, 0, 1), (in_back, 0, 3), (z_finish, 4), (attend_back, 0, 2, 1),
        (project_back, 0, 2), (heads_grad, 0, 1), (attend_back, 0, 1, 2), (mid_back, 0, 0), (attend_back, 0, 1, 1),
        (z_start, 6), (attend_back, 0, 1, 0), (project_back, 0, 1), (in_back, 0, 2), (heads_grad, 0, 0),
        (attend_back, 0, 0, 2), (attend_back, 0, 0, 1), (attend_back, 0, 0, 0), (project_back, 0, 0),
        (grads_attend, 0), (z_finish, 5), (in_back, 0, 1), (block_back, 0, 3), (in_back, 0, 0), (small_0,),
        (block_back, 0, 2), (z_start, 7), (small_1,), (block_back, 0, 1), (z_finish, 6), (block_back, 0, 0),
        (small_2,), (current_back,), (z_start, 8), (z_finish, 7), (z_start, 9), (z_finish, 8), (z_start, 10),
        (z_finish, 9), (z_start, 11), (small_3,), (z_finish, 10), (z_finish, 11), (small_4,),
    ]
    for task, *where in order:
        task(*where)

    if not inner:
        out = pltpu.make_async_copy(r.grads, r.raw, r.load_sem.at[0])
        out.start()
        out.wait()


def finish(names, past, *refs):
    r = types.SimpleNamespace(**dict(zip(names, refs)))
    grad, grad_next = r.cotangent[...].astype(F32), r.grad_next_t[...]
    for j in range(past):
        r.grad_history[j] = (r.first[j] * grad_next + r.second[j] * grad).astype(BF16)
    r.mixed[...] = r.mixed_t[...]
    r.grad_current[...] = r.grad_current_t[...]
    width = r.grad_gain_attn.shape[1]
    for i in range(width // 128):
        lanes = slice(i * 128, (i + 1) * 128)
        r.grad_gain_attn[:, lanes] = r.sums[4 * i : 4 * i + 2, :]
        r.grad_gain_mlp[:, lanes] = r.sums[4 * i + 2 : 4 * i + 4, :]
    base = width // 32
    dots = r.sums[base : base + 32, :]
    for j in range(past + 1):
        r.grad_first[j] = dots[j, 0]
    for j in range(past + 2):
        r.grad_second[j] = dots[16 + j, 0]
    half, own_width = width // 2, width // 4
    for l in (0, 1):
        first = 6 * (1 - l)
        for i in (0, 1):
            lanes = slice(i * half, (i + 1) * half)
            r.grad_down[l, :, lanes] = r.parts[first + i]
            r.grad_up[l, :, lanes] = r.parts[first + 2 + i]
        r.grad_qkv[l, :, :half] = r.parts[first + 4]
        r.grad_qkv[l, :, half:] = r.parts[first + 5, :, :own_width]
        r.grad_out[l] = r.parts[first + 5, :, own_width:].T


def tables(rows):
    freqs = 10000.0 ** (-2.0 * np.arange(HEAD // 2) / HEAD)
    angles = np.arange(rows)[:, None] * np.tile(freqs, 4)[None, :]
    return np.cos(angles).astype(np.float32), np.sin(angles).astype(np.float32)


def shards(
    n_dp,
    current,
    history,
    cotangent,
    seq_lengths,
    w_qkv,
    w_out,
    w_up,
    w_down,
    gain_attn,
    gain_mlp,
    dwa_first,
    dwa_second,
):
    rows, own_width = current.shape
    past = history.shape[0]
    layers, width, _ = w_qkv.shape
    heads = w_out.shape[1] // HEAD
    units = w_up.shape[2]
    count = CHUNKS
    sub, half, block = rows // (2 * count), width // 2, width // 8
    inner = n_dp == 8
    cos_table, sin_table = tables(rows)

    hbm = pl.BlockSpec(memory_space=pl.ANY)
    vmem = pl.BlockSpec(memory_space=pltpu.VMEM)
    smem = pl.BlockSpec(memory_space=pltpu.SMEM)
    inputs = dict(
        current=(current.T, hbm),
        history=(history.transpose(0, 2, 1), hbm),
        cotangent=(cotangent.T, hbm),
        seq=(seq_lengths, smem),
        w_qkv=(w_qkv.transpose(0, 2, 1), hbm),
        w_out=(w_out, hbm),
        w_up=(w_up, hbm),
        w_down=(w_down, hbm),
        gain_attn=(gain_attn, vmem),
        gain_mlp=(gain_mlp, vmem),
        first=(dwa_first, smem),
        second=(dwa_second, smem),
        cos_table=(jnp.asarray(cos_table), hbm),
        sin_table=(jnp.asarray(sin_table), hbm),
    )

    def shape(dims, kind):
        return jax.ShapeDtypeStruct(dims, kind)

    small_rows = width // 32 + 32
    outputs = dict(
        mixed_t=(shape((own_width, rows), BF16), vmem),
        grad_current_t=(shape((own_width, rows), BF16), vmem),
        grad_next_t=(shape((own_width, rows), F32), vmem),
        sums=(shape((small_rows, 128), F32), vmem),
    )
    if inner:
        outputs.update(
            parts=(shape((6 * layers, block, half), F32), vmem),
        )
    else:
        outputs.update(
            raw=(shape((6 * layers, 2, 4, block, half), BF16), hbm),
        )

    def whole(kind=BF16, *lead):
        return pltpu.VMEM((*lead, rows, width), kind)

    def quarter(kind, *lead):
        return pltpu.VMEM((*lead, sub, width), kind)

    def quarter_half(kind, *lead):
        return pltpu.VMEM((*lead, sub, half), kind)

    def quarter_own(kind, *lead):
        return pltpu.VMEM((*lead, sub, own_width), kind)

    dma = pltpu.SemaphoreType.DMA
    scratch = dict(
        cur=pltpu.VMEM((rows, own_width), BF16),
        cot=pltpu.VMEM((rows, own_width), BF16),
        rope_cos=pltpu.VMEM((rows, 128), F32),
        rope_sin=pltpu.VMEM((rows, 128), F32),
        bias=pltpu.VMEM((rows, rows), BF16),
        wq=pltpu.VMEM((layers, 3 * own_width, width), BF16),
        wo=pltpu.VMEM(w_out.shape, BF16),
        wu=pltpu.VMEM(w_up.shape, BF16),
        wd=pltpu.VMEM(w_down.shape, BF16),
        cur_t=pltpu.VMEM((own_width, rows), BF16),
        cot_t=pltpu.VMEM((own_width, rows), BF16),
        hist=pltpu.VMEM((past, own_width, rows), BF16),
        blend1=pltpu.VMEM((rows, own_width), F32),
        blend2_t=pltpu.VMEM((own_width, rows), F32),
        grad_next=pltpu.VMEM((rows, own_width), F32),
        blend1_home=quarter_half(F32, count),
        home=quarter_half(F32),
        cot_home=quarter_half(BF16, count),
        y0=quarter_half(F32, count),
        xs=quarter(BF16, layers, count),
        z1=quarter(BF16, layers, count),
        z2=quarter(BF16, layers, count),
        s1=pltpu.VMEM((layers, count, sub, 1), F32),
        s2=pltpu.VMEM((layers, count, sub, 1), F32),
        acc=quarter(F32, count),
        mid=quarter_half(F32, count),
        n1=whole(BF16, layers),
        n2=whole(BF16, layers),
        hid=pltpu.VMEM((layers, rows, units), BF16),
        slope=pltpu.VMEM((layers, rows, units), BF16),
        gp=pltpu.VMEM((rows, units), BF16),
        gy=whole(),
        gm=whole(),
        q=pltpu.VMEM((layers, heads, rows, HEAD), BF16),
        k=pltpu.VMEM((layers, heads, rows, HEAD), BF16),
        v=pltpu.VMEM((layers, heads, rows, HEAD), BF16),
        att=pltpu.VMEM((layers, rows, own_width), BF16),
        lse=pltpu.VMEM((layers, rows, heads), F32),
        dqk=pltpu.VMEM((heads, rows, 2 * HEAD), F32),
        dv=pltpu.VMEM((rows, own_width), F32),
        dqkv=pltpu.VMEM((rows, 3 * own_width), BF16),
        gains=pltpu.VMEM((8, width), F32),
        dots=pltpu.VMEM((32, rows), F32),
        small=pltpu.VMEM((4, small_rows, 128), F32),
        small_in=pltpu.VMEM((6, small_rows, 128), F32),
        cstage=quarter(BF16, count),
        crecv_fwd=quarter(BF16, count),
        crecv_bwd=quarter(BF16, count),
        xstage=quarter(BF16, count),
        xrecv_whole=quarter(BF16, count),
        xstage_half=quarter_half(BF16, count),
        xrecv_half=quarter_half(BF16, count),
        cv_cur=quarter_own(BF16, count),
        cv_wide=quarter_own(F32, count),
        cs_wide=quarter_own(F32, count),
        grad_att=pltpu.VMEM((rows, own_width), BF16),
        cv_cot=quarter_own(BF16, count),
        cs_gc=quarter_own(BF16, count),
        cv_gc=quarter_own(BF16, count),
        grads=pltpu.VMEM((6 * layers, 2, 4, block, half), BF16),
        load_sem=dma((8,)),
        hist_in=dma((4,)),
        core_send=dma((14, count)),
        core_recv=dma((14, count)),
        x_send=dma((6, count)),
        x_recv=dma((6, count)),
    )
    if inner:
        scratch.update(
            y_in=pltpu.VMEM((6 * layers, 4, block, half), BF16),
            z_in=pltpu.VMEM((6 * layers, 3, block, half), BF16),
            y_send=dma((6 * layers,)),
            y_recv=dma((6 * layers,)),
            z_send=dma((6 * layers, 3)),
            z_recv=dma((6 * layers, 3)),
            sm_send=dma((6,)),
            sm_recv=dma((6,)),
        )
    names = [*inputs, *outputs, *scratch]
    results = pl.pallas_call(
        functools.partial(kernel, names, (rows, width, heads, units, past, count, inner)),
        out_shape=[o[0] for o in outputs.values()],
        in_specs=[i[1] for i in inputs.values()],
        out_specs=[o[1] for o in outputs.values()],
        scratch_shapes=[*scratch.values()],
        compiler_params=pltpu.CompilerParams(
            collective_id=0, has_side_effects=True, vmem_limit_bytes=int(63.5 * 2**20)
        ),
    )(*[i[0] for i in inputs.values()])
    out = types.SimpleNamespace(**dict(zip(outputs, results)))
    if not inner:
        out.sums = lax.psum(out.sums, ("dp", "mp"))

        raw = out.raw.transpose(0, 2, 1, 3, 4).reshape(6 * layers, width, half).astype(F32)
        out.parts = lax.psum_scatter(raw, "dp", scatter_dimension=1, tiled=True)
    share = out.parts.shape[1]
    given = dict(
        cotangent=(cotangent.T, vmem),
        first=(dwa_first, smem),
        second=(dwa_second, smem),
        mixed_t=(out.mixed_t, vmem),
        grad_current_t=(out.grad_current_t, vmem),
        grad_next_t=(out.grad_next_t, vmem),
        sums=(out.sums, vmem),
        parts=(out.parts, vmem),
    )
    wanted = dict(
        mixed=(shape((own_width, rows), BF16), vmem),
        grad_current=(shape((own_width, rows), BF16), vmem),
        grad_history=(shape((past, own_width, rows), BF16), vmem),
        grad_qkv=(shape((layers, share, 3 * own_width), F32), vmem),
        grad_out=(shape((layers, own_width, share), F32), vmem),
        grad_up=(shape((layers, share, units), F32), vmem),
        grad_down=(shape((layers, share, units), F32), vmem),
        grad_gain_attn=(shape((layers, width), F32), vmem),
        grad_gain_mlp=(shape((layers, width), F32), vmem),
        grad_first=(shape((past + 1,), F32), smem),
        grad_second=(shape((past + 2,), F32), smem),
    )
    results = pl.pallas_call(
        functools.partial(finish, [*given, *wanted], past),
        out_shape=[o[0] for o in wanted.values()],
        in_specs=[i[1] for i in given.values()],
        out_specs=[o[1] for o in wanted.values()],
        compiler_params=pltpu.CompilerParams(vmem_limit_bytes=62 * 2**20),
    )(*[i[0] for i in given.values()])
    out = types.SimpleNamespace(**dict(zip(wanted, results)))
    return (
        out.mixed.T,
        out.grad_current.T,
        out.grad_history.transpose(0, 2, 1),
        out.grad_qkv,
        out.grad_out,
        out.grad_up,
        out.grad_down.transpose(0, 2, 1),
        out.grad_gain_attn,
        out.grad_gain_mlp,
        out.grad_first,
        out.grad_second,
    )


def solution(mesh):
    in_specs = (
        P("dp", "mp"),
        P(None, "dp", "mp"),
        P("dp", "mp"),
        P("dp", None),
        P(None, None, "mp"),
        P(None, "mp", None),
        P(None, None, "mp"),
        P(None, "mp", None),
        P(),
        P(),
        P(),
        P(),
    )
    out_specs = (
        P("dp", "mp"),
        P("dp", "mp"),
        P(None, "dp", "mp"),
        P(None, "dp", "mp"),
        P(None, "mp", "dp"),
        P(None, "dp", "mp"),
        P(None, "mp", "dp"),
        P(),
        P(),
        P(),
        P(),
    )
    return jax.shard_map(
        functools.partial(shards, mesh.shape["dp"]),
        mesh=mesh,
        in_specs=in_specs,
        out_specs=out_specs,
        check_vma=False,
    )
```
